32 devices in a mesh: grp: 2 (over y), tm: 4 (over z), chan: 4 (over x, core).
Axes of the slice: x: 2, y: 2, z: 4, core: 2. Of those that a mesh axis runs over, the one named last changes fastest.
Arguments:
- voltages: int32 [512, 65536], P(('grp', 'chan'), 'tm'), parts along dimension 0, may hold values from -128 to 127
- beam_delays: int32 [256, 256], replicated, may hold values from 0 to 4095
- cal_gains: float32 [2, 4096, 256], P(None, ('grp', 'tm', 'chan')), parts along dimension 1, may hold values from -4 to 4
Outputs:
- visibilities: bfloat16 [2, 4096, 256, 256], P(None, ('grp', 'tm', 'chan')), parts along dimension 1
- beam_power: bfloat16 [4096, 16, 256], P(('grp', 'tm', 'chan')), parts along dimension 0
The draws below stay inside these ranges and needn't reach their ends.
There are 2 independent parts, one for each index of `grp`. The reference program is written for one: setup_inputs(seed, part) draws one part's arguments, and reference() takes and returns one part's arrays. A program takes and returns all parts, laid end to end along the dimension named above; an argument that names none is the same for every part. Nothing has to cross between parts.
All inputs are finite; a program needn't handle non-finite values.
Results may differ from the reference program's by a relative error of at most 0.0062.
Values may be sent and summed in bfloat16 or wider, within the bound.
No kernel may reach another device: no remote copies, remote signals or barrier semaphores. Data moves between devices by JAX's collectives and lax.ppermute only.
A program may use at most 192 MiB of HBM per device.

```python
import math
import jax
import jax.numpy as jnp
from jax import lax

INP = 256
BEAMS = 256
TAPS = 4
SPEC_DEV = 4
NFFT = 4096
CH = 2048
SAMPLES = 65536
N_TM = 4


def plant(values, key, low, high):
    shape = values.shape
    place = [jax.random.randint(jax.random.fold_in(key, axis), (), 0, shape[axis]) for axis in range(len(shape))]
    values = values.at[tuple(place)].set(low)
    longest = shape.index(max(shape))
    place[longest] = (place[longest] + 1) % shape[longest]
    return values.at[tuple(place)].set(high)


def shard_levels(rng, shape, pieces, low, high):
    def one(axis_at, blocks):
        heights = jax.random.uniform(jax.random.fold_in(jax.random.fold_in(rng, 6), axis_at), (blocks,), jnp.float32, low / len(pieces), high / len(pieces))
        return jnp.repeat(jnp.exp(heights), shape[axis_at] // blocks).reshape((-1,) + (1,) * (len(shape) - axis_at - 1))

    factor_of = one(*pieces[0])
    for cut in pieces[1:]:
        factor_of = factor_of * one(*cut)
    return factor_of


def noise(rng, extent, deviation, bound, pieces=(), kind=jnp.bfloat16):
    values = deviation * jax.random.normal(rng, extent, jnp.float32)
    if pieces:
        values = values * shard_levels(rng, extent, pieces, -0.22, 0.18)
    return jnp.clip(values, -bound, bound).astype(kind)


def setup_inputs(seed: int = 0, part: int = 0) -> dict:
    key_list = jax.random.split(jax.random.key(seed), 4)
    own_keys = jax.random.split(jax.random.fold_in(key_list[3], part), 4)
    voltages = plant(jax.random.randint(own_keys[0], (INP, SAMPLES), -128, 128), jax.random.fold_in(own_keys[0], 1), -128, 127).astype(jnp.int32)
    beam_delays = plant(jax.random.randint(key_list[1], (BEAMS, INP), 0, NFFT), jax.random.fold_in(key_list[1], 1), 0, NFFT - 1).astype(jnp.int32)
    cal_gains = noise(own_keys[2], (2, CH, INP), 0.7, 4.0, ((1, 16),), jnp.float32)
    return dict(voltages=voltages, beam_delays=beam_delays, cal_gains=cal_gains)


def pfb_window():
    total_len = TAPS * NFFT
    sample_pos = jnp.arange(total_len, dtype=jnp.float32)
    centre = (sample_pos - total_len / 2 + 0.5) / NFFT
    taper_win = 0.5 - 0.5 * jnp.cos(2.0 * math.pi * (sample_pos + 0.5) / total_len)
    coeffs = jnp.sinc(centre) * taper_win
    coeffs = coeffs / jnp.sqrt(jnp.sum(coeffs * coeffs))
    return coeffs.reshape(TAPS, NFFT)

def reference(voltages, beam_delays, cal_gains):
    spectra_total = SPEC_DEV * N_TM
    coeffs = pfb_window()
    samples = voltages.astype(jnp.float32).reshape(INP, spectra_total, NFFT)
    padded = jnp.concatenate([samples, jnp.zeros((INP, TAPS - 1, NFFT), jnp.float32)], axis=1)
    in_block = 16
    padded = padded.reshape(INP // in_block, in_block, spectra_total + TAPS - 1, NFFT)

    def channelize(block_in):
        filtered = coeffs[0] * block_in[:, 0:spectra_total]
        for tap_index in range(1, TAPS):
            filtered = filtered + coeffs[tap_index] * block_in[:, tap_index:tap_index + spectra_total]
        freq = jnp.fft.rfft(filtered, axis=-1)[..., :CH] * (1.0 / 64.0)
        return (jnp.real(freq).astype(jnp.bfloat16), jnp.imag(freq).astype(jnp.bfloat16))
    spec_re, spec_im = lax.map(channelize, padded)
    spec_re = spec_re.reshape(INP, spectra_total, CH).transpose(2, 1, 0)
    spec_im = spec_im.reshape(INP, spectra_total, CH).transpose(2, 1, 0)
    ch_block = 64
    n_blocks = CH // ch_block
    chan_index = jnp.arange(CH, dtype=jnp.int32).reshape(n_blocks, ch_block)
    weight_norm = 1.0 / math.sqrt(INP)

    def correlate(packed):
        z_re, z_im, g_re, g_im, chan_ids = packed
        a_re = z_re.astype(jnp.float32)
        a_im = z_im.astype(jnp.float32)
        g_re = g_re[:, None, :]
        g_im = g_im[:, None, :]
        cal_re = (g_re * a_re - g_im * a_im).astype(jnp.bfloat16).astype(jnp.float32)
        cal_im = (g_re * a_im + g_im * a_re).astype(jnp.bfloat16).astype(jnp.float32)
        stacked = jnp.concatenate([cal_re, cal_im], axis=1)
        flipped = jnp.concatenate([cal_im, -cal_re], axis=1)
        vis_re = jnp.einsum('ctp,ctq->cpq', stacked, stacked)
        vis_im = jnp.einsum('ctp,ctq->cpq', flipped, stacked)
        vis_out = (jnp.stack([vis_re, vis_im]) / spectra_total).astype(jnp.bfloat16)
        phase_idx = beam_delays[None, :, :] * chan_ids[:, None, None] % NFFT
        angles = phase_idx.astype(jnp.float32) * (2.0 * math.pi / NFFT)
        weight_re = (jnp.cos(angles) * weight_norm).astype(jnp.bfloat16).astype(jnp.float32)
        weight_im = (-jnp.sin(angles) * weight_norm).astype(jnp.bfloat16).astype(jnp.float32)
        beam_re = jnp.einsum('cti,cbi->ctb', cal_re, weight_re) - jnp.einsum('cti,cbi->ctb', cal_im, weight_im)
        beam_im = jnp.einsum('cti,cbi->ctb', cal_im, weight_re) + jnp.einsum('cti,cbi->ctb', cal_re, weight_im)
        power_out = (beam_re * beam_re + beam_im * beam_im).astype(jnp.bfloat16)
        return (vis_out, power_out)
    vis_all, power_all = lax.map(correlate, (spec_re.reshape(n_blocks, ch_block, spectra_total, INP), spec_im.reshape(n_blocks, ch_block, spectra_total, INP), cal_gains[0].reshape(n_blocks, ch_block, INP), cal_gains[1].reshape(n_blocks, ch_block, INP), chan_index))
    visibilities = vis_all.transpose(1, 0, 2, 3, 4).reshape(2, CH, INP, INP)
    beam_power = power_all.reshape(CH, spectra_total, BEAMS)
    return (visibilities, beam_power)
```

```python
import functools
import math

import jax
import jax.numpy as jnp
import numpy as np
from jax import lax
from jax.experimental import pallas as pl
from jax.experimental.pallas import tpu as pltpu
from jax.sharding import PartitionSpec as P

TAPS = 4
FA = 64
FB = 64
NFFT = 4096
CH = 2048
RAD = 32
LANES = 128
PAIRS = RAD // 2
ROWS = NFFT // PAIRS
CHAN_BLOCK = 8
ROT = 16
MIB = 1 << 20


def shifted(block, axis, distance):
    devices = range(lax.axis_size(axis))
    route = [(i - distance, i) for i in devices if i - distance in devices]
    return lax.ppermute(block, axis, route)


def window_table():
    total_len = TAPS * NFFT
    pos = np.arange(total_len, dtype=np.float64)
    centre = (pos - total_len / 2 + 0.5) / NFFT
    taper = 0.5 - 0.5 * np.cos(2.0 * np.pi * (pos + 0.5) / total_len)
    coeffs = np.sinc(centre) * taper
    coeffs = coeffs / np.sqrt(np.sum(coeffs * coeffs))
    return coeffs.reshape(TAPS, NFFT).astype(np.float32)


def split_table(table):
    high = table.astype(jnp.bfloat16)
    low = (table - high.astype(np.float64)).astype(jnp.bfloat16)
    return high, low


def second_tables():
    lane = np.arange(LANES)
    k1 = np.arange(CH // RAD)
    table = np.zeros((PAIRS, CH // RAD, 2, 2, 2, LANES))
    for m in range(PAIRS):
        if m == 0:
            for which, k2 in enumerate((0, RAD // 2)):
                phase = (RAD * k1[:, None] + k2) * lane[None, :] % NFFT
                angle = 2.0 * np.pi * phase / NFFT
                table[m, :, which, 0, which] = np.cos(angle)
                table[m, :, which, 1, which] = -np.sin(angle)
            continue
        for which in range(2):
            channel = RAD * k1 + (m if which == 0 else RAD - m)
            source = channel if which == 0 else NFFT - channel
            sign = 1.0 if which == 0 else -1.0
            angle = 2.0 * np.pi * (source[:, None] * lane[None, :] % NFFT) / NFFT
            cos, sin = np.cos(angle), np.sin(angle)
            table[m, :, which, 0, 0] = cos
            table[m, :, which, 0, 1] = sin
            table[m, :, which, 1, 0] = -sin * sign
            table[m, :, which, 1, 1] = cos * sign
    return split_table(table.reshape(PAIRS, ROWS, 2 * LANES) / 64.0)


def real_transform(vals):
    n = len(vals)
    if n == 2:
        return [(vals[0] + vals[1], None), (vals[0] - vals[1], None)]
    even = real_transform(vals[0::2])
    odd = real_transform(vals[1::2])
    half = n // 2
    out = [None] * (half + 1)
    out[0] = (even[0][0] + odd[0][0], None)
    out[half] = (even[0][0] - odd[0][0], None)
    for k in range(1, n // 4):
        c, s = math.cos(2 * math.pi * k / n), math.sin(2 * math.pi * k / n)
        (er, ei), (sr, si) = even[k], odd[k]
        if 8 * k == n:
            tr, ti = (sr + si) * c, (si - sr) * c
        else:
            tr, ti = sr * c + si * s, si * c - sr * s
        out[k] = (er + tr, ei + ti)
        out[half - k] = (er - tr, ti - ei)
    out[n // 4] = (even[n // 4][0], -odd[n // 4][0])
    return out


def spectra_kernel(spec, rows_in, steps_in, pairs, x_ref, halo_ref, win_ref, high_ref, low_ref, out_ref, wide, mid):
    step = pl.program_id(0)

    @pl.when(step < steps_in)
    def _():
        own = spec * NFFT
        wide[:, :own] = x_ref[...].astype(jnp.float32)
        wide[:, own:] = halo_ref[...].astype(jnp.float32)
        inputs = rows_in * steps_in

        @pl.loop(0, rows_in // 8)
        def _(sub):
            rows = pl.ds(pl.multiple_of(sub * 8, 8), 8)
            for s in range(spec):
                vals = []
                for col in range(RAD):
                    total = None
                    for tap in range(TAPS):
                        at = (s + tap) * NFFT + col * LANES
                        term = wide[rows, at : at + LANES] * win_ref[tap : tap + 1, col * LANES : (col + 1) * LANES]
                        total = term if total is None else total + term
                    vals.append(total)
                freq = real_transform(vals)
                place = pl.ds(pl.multiple_of(s * inputs + step * rows_in + sub * 8, 8), 8)
                mid[0, place, :LANES] = freq[0][0]
                mid[0, place, LANES:] = freq[PAIRS][0]
                for m in range(1, PAIRS):
                    mid[m, place, :LANES] = freq[m][0]
                    mid[m, place, LANES:] = freq[m][1]

    @pl.when(step >= steps_in)
    def _():
        first = (step - steps_in) * pairs
        owners, _, lanes = out_ref.shape
        per = ROWS // owners
        for p in range(pairs):
            both = mid[first + p]
            high = both.astype(jnp.bfloat16)
            low = (both - high.astype(jnp.float32)).astype(jnp.bfloat16)
            left = jnp.concatenate([high_ref[p], high_ref[p], low_ref[p]], axis=1)
            right = jnp.concatenate([high, low, high], axis=1)
            total = lax.dot_general(left, right, (((1,), (1,)), ((), ())), preferred_element_type=jnp.float32)
            out_ref[:, p * per : (p + 1) * per, :] = total.reshape(owners, per, lanes).astype(jnp.bfloat16)


def spectra(voltages, halo, owners):
    inputs = voltages.shape[0]
    spec = voltages.shape[1] // NFFT
    lanes = inputs * spec
    rows_in, pairs = 16, 4
    steps_in, steps_out = inputs // rows_in, PAIRS // pairs
    per = ROWS // owners
    high, low = second_tables()
    before = lambda g: jnp.minimum(g, steps_in - 1)
    after = lambda g: jnp.maximum(g - steps_in, 0)
    return pl.pallas_call(
        functools.partial(spectra_kernel, spec, rows_in, steps_in, pairs),
        grid=(steps_in + steps_out,),
        in_specs=[
            pl.BlockSpec((rows_in, spec * NFFT), lambda g: (before(g), 0)),
            pl.BlockSpec((rows_in, (TAPS - 1) * NFFT), lambda g: (before(g), 0)),
            pl.BlockSpec((TAPS, NFFT), lambda g: (0, 0)),
            pl.BlockSpec((pairs, ROWS, 2 * LANES), lambda g: (after(g), 0, 0)),
            pl.BlockSpec((pairs, ROWS, 2 * LANES), lambda g: (after(g), 0, 0)),
        ],
        out_specs=pl.BlockSpec((owners, pairs * per, lanes), lambda g: (0, after(g), 0)),
        out_shape=jax.ShapeDtypeStruct((owners, PAIRS * per, lanes), jnp.bfloat16),
        scratch_shapes=[
            pltpu.VMEM((rows_in, (spec + TAPS - 1) * NFFT), jnp.float32),
            pltpu.VMEM((PAIRS, lanes, 2 * LANES), jnp.float32),
        ],
        compiler_params=pltpu.CompilerParams(vmem_limit_bytes=40 * MIB),
        cost_estimate=pl.CostEstimate(flops=6 * PAIRS * ROWS * 256 * lanes, bytes_accessed=12 * MIB, transcendentals=0),
        name="spectra",
    )(voltages, halo, jnp.asarray(window_table()), jnp.asarray(high), jnp.asarray(low))


def unit_circle(phase):
    quarter = NFFT // 4
    quad = (phase + quarter // 2) // quarter
    x = (phase - quad * quarter).astype(jnp.float32) * (2.0 * math.pi / NFFT)
    q = x * x
    cos = 1.0 + q * (-1 / 2 + q * (1 / 24 + q * (-1 / 720 + q * (1 / 40320))))
    sin = x * (1.0 + q * (-1 / 6 + q * (1 / 120 + q * (-1 / 5040 + q * (1 / 362880)))))
    odd = quad % 2 == 1
    c, s = jnp.where(odd, sin, cos), jnp.where(odd, cos, sin)
    c = jnp.where((quad == 1) | (quad == 2), -c, c)
    s = jnp.where((quad == 2) | (quad == 3), -s, s)
    return c, s


def weights_kernel(norm, first_ref, delay_ref, out_ref):
    delays = delay_ref[...]
    step_cos, step_sin = unit_circle(delays)

    @pl.loop(0, out_ref.shape[0] // ROT)
    def _(group):
        c, s = unit_circle(delays * (first_ref[0] + group * ROT) % NFFT)
        c, s = c * norm, s * -norm
        for j in range(ROT):
            k = group * ROT + j
            out_ref[k, 0] = c.astype(jnp.bfloat16)
            out_ref[k, 1] = s.astype(jnp.bfloat16)
            if j + 1 < ROT:
                c, s = c * step_cos + s * step_sin, s * step_cos - c * step_sin


def beam_weights(beam_delays, chan_first, chan_local):
    beams, inputs = beam_delays.shape
    rows = 16
    return pl.pallas_call(
        functools.partial(weights_kernel, 1.0 / math.sqrt(inputs)),
        grid=(inputs // rows,),
        in_specs=[
            pl.BlockSpec(memory_space=pltpu.SMEM),
            pl.BlockSpec((rows, beams), lambda g: (g, 0)),
        ],
        out_specs=pl.BlockSpec((chan_local, 2, rows, beams), lambda g: (0, 0, g, 0)),
        out_shape=jax.ShapeDtypeStruct((chan_local, 2, inputs, beams), jnp.bfloat16),
        compiler_params=pltpu.CompilerParams(vmem_limit_bytes=24 * MIB),
        cost_estimate=pl.CostEstimate(
            flops=60 * chan_local * inputs * beams, bytes_accessed=4 * chan_local * inputs * beams, transcendentals=0
        ),
        name="weights",
    )(chan_first.reshape(1), beam_delays.T)


def combine_kernel(tm_count, spec, inputs, g_ref, gain_ref, w_ref, vis_ref, power_ref, rows_ref):
    step = pl.program_id(0)
    rows = g_ref.shape[1]
    per = rows // PAIRS
    times = tm_count * spec
    half = LANES // 2

    @pl.when(step == 0)
    def _():
        low_half = lax.broadcasted_iota(jnp.int32, (per, LANES), 1) < half

        @pl.loop(0, PAIRS)
        def _(m):
            at = pl.ds(pl.multiple_of(m * per, per), per)
            for t in range(tm_count):
                for pair in range(2):
                    for two in range(2):
                        cols = slice(two * LANES, (two + 1) * LANES)
                        a = g_ref[t * 4 + 2 * pair, at, cols].astype(jnp.float32)
                        b = g_ref[t * 4 + 2 * pair + 1, at, cols].astype(jnp.float32)
                        even = jnp.where(low_half, a, pltpu.roll(b, half, 1))
                        odd = jnp.where(low_half, pltpu.roll(a, half, 1), b)
                        s = t * spec + 2 * two
                        rows_ref[pair, pl.ds(pl.multiple_of(s * rows + m * per, per), per), :] = even
                        rows_ref[pair, pl.ds(pl.multiple_of((s + 1) * rows + m * per, per), per), :] = odd

    scale = 1.0 / times
    blocks = RAD // CHAN_BLOCK
    for u in range(CHAN_BLOCK):
        k = step * CHAN_BLOCK + u
        k2 = (step % blocks) * CHAN_BLOCK + u
        upper = k2 // PAIRS
        m = jnp.where(k2 == PAIRS, 0, jnp.where(upper == 1, RAD - k2, k2))
        row = m * per + (step // blocks) * 4 + upper * 2
        z_re = jnp.concatenate([rows_ref[p, pl.ds(row, times, stride=rows), :] for p in range(2)], axis=1)
        z_im = jnp.concatenate([rows_ref[p, pl.ds(row + 1, times, stride=rows), :] for p in range(2)], axis=1)
        g_re = gain_ref[0, u : u + 1, :]
        g_im = gain_ref[1, u : u + 1, :]
        cal_re = (g_re * z_re - g_im * z_im).astype(jnp.bfloat16)
        cal_im = (g_re * z_im + g_im * z_re).astype(jnp.bfloat16)
        stacked = jnp.concatenate([cal_re, cal_im], axis=0)
        turned = jnp.concatenate([-cal_im, cal_re], axis=0)
        both = jnp.concatenate([stacked, turned], axis=1)
        vis = lax.dot_general(stacked, both, (((0,), (0,)), ((), ())), preferred_element_type=jnp.float32)
        vis = (vis * scale).astype(jnp.bfloat16)
        vis_ref[0, u] = vis[:, :inputs]
        vis_ref[1, u] = vis[:, inputs:]
        left = jnp.concatenate([stacked, turned], axis=1)
        w = w_ref[u].reshape(2 * inputs, w_ref.shape[3])
        formed = lax.dot_general(left, w, (((1,), (0,)), ((), ())), preferred_element_type=jnp.float32)
        formed = formed * formed
        power_ref[u] = (formed[:times] + formed[times:]).astype(jnp.bfloat16)


def combine(gathered, cal_gains, weights, tm_count, spec):
    sources, rows, lanes = gathered.shape
    chan_local, _, inputs, beams = weights.shape
    times = tm_count * spec
    return pl.pallas_call(
        functools.partial(combine_kernel, tm_count, spec, inputs),
        grid=(chan_local // CHAN_BLOCK,),
        in_specs=[
            pl.BlockSpec((sources, rows, lanes), lambda g: (0, 0, 0)),
            pl.BlockSpec((2, CHAN_BLOCK, inputs), lambda g: (0, g, 0)),
            pl.BlockSpec((CHAN_BLOCK, 2, inputs, beams), lambda g: (g, 0, 0, 0)),
        ],
        out_specs=[
            pl.BlockSpec((2, CHAN_BLOCK, inputs, inputs), lambda g: (0, g, 0, 0)),
            pl.BlockSpec((CHAN_BLOCK, times, beams), lambda g: (g, 0, 0)),
        ],
        out_shape=[
            jax.ShapeDtypeStruct((2, chan_local, inputs, inputs), jnp.bfloat16),
            jax.ShapeDtypeStruct((chan_local, times, beams), jnp.bfloat16),
        ],
        scratch_shapes=[pltpu.VMEM((2, times * rows, LANES), jnp.float32)],
        compiler_params=pltpu.CompilerParams(vmem_limit_bytes=40 * MIB),
        cost_estimate=pl.CostEstimate(
            flops=chan_local * (4 * 2 * times * inputs * inputs + 8 * times * inputs * beams),
            bytes_accessed=chan_local * (4 * inputs * inputs + 4 * inputs * beams),
            transcendentals=0,
        ),
        name="combine",
    )(gathered, cal_gains, weights)


def fits(voltages, beam_delays, tm_count, chan_count):
    inp_dev, samples = voltages.shape
    spec = samples // NFFT
    owners = tm_count * chan_count
    return (
        ROWS % owners == 0
        and ROWS // owners == 16
        and spec == 4
        and chan_count == 4
        and inp_dev * 2 == LANES
        and beam_delays.shape[1] == inp_dev * chan_count
    )


def shards(voltages, beam_delays, cal_gains):
    tm_count = lax.axis_size("tm")
    chan_count = lax.axis_size("chan")
    if not fits(voltages, beam_delays, tm_count, chan_count):
        return plain_shards(voltages, beam_delays, cal_gains)
    owners = tm_count * chan_count
    chan_local = CH // owners
    spec_dev = voltages.shape[1] // NFFT
    halo = shifted(voltages[:, : (TAPS - 1) * NFFT].astype(jnp.bfloat16), "tm", -1)
    chan_first = (lax.axis_index("tm") * chan_count + lax.axis_index("chan")) * chan_local
    weights = beam_weights(beam_delays, chan_first, chan_local)
    sent = spectra(voltages, halo, owners)
    gathered = lax.all_to_all(sent, ("tm", "chan"), split_axis=0, concat_axis=0, tiled=True)
    visibilities, beam_power = combine(gathered, cal_gains, weights, tm_count, spec_dev)
    return (visibilities, beam_power)


def pfb_window():
    total_len = TAPS * NFFT
    sample_pos = jnp.arange(total_len, dtype=jnp.float32)
    centre = (sample_pos - total_len / 2 + 0.5) / NFFT
    taper_win = 0.5 - 0.5 * jnp.cos(2.0 * math.pi * (sample_pos + 0.5) / total_len)
    coeffs = jnp.sinc(centre) * taper_win
    coeffs = coeffs / jnp.sqrt(jnp.sum(coeffs * coeffs))
    return coeffs.reshape(TAPS, NFFT)


def phase_table(left, right, modulus):
    phase_idx = left[:, None] * right[None, :] % modulus
    angles = phase_idx.astype(jnp.float32) * (2.0 * math.pi / modulus)
    return (jnp.cos(angles), jnp.sin(angles))


def transform(row_block):
    best = lax.Precision.HIGHEST
    first_idx = jnp.arange(FA, dtype=jnp.int32)
    second_idx = jnp.arange(FB, dtype=jnp.int32)
    half_idx = jnp.arange(FB // 2, dtype=jnp.int32)
    cos_one, sin_one = phase_table(first_idx, first_idx, FA)
    section_re = jnp.einsum("rab,ak->rkb", row_block, cos_one, precision=best)
    section_im = -jnp.einsum("rab,ak->rkb", row_block, sin_one, precision=best)
    twid_cos, twid_sin = phase_table(first_idx, second_idx, NFFT)
    inner_re = section_re * twid_cos + section_im * twid_sin
    inner_im = section_im * twid_cos - section_re * twid_sin
    cos_two, sin_two = phase_table(second_idx, half_idx, FB)
    freq_re = jnp.einsum("rkb,bq->qkr", inner_re, cos_two, precision=best) + jnp.einsum(
        "rkb,bq->qkr", inner_im, sin_two, precision=best
    )
    freq_im = jnp.einsum("rkb,bq->qkr", inner_im, cos_two, precision=best) - jnp.einsum(
        "rkb,bq->qkr", inner_re, sin_two, precision=best
    )
    row_count = row_block.shape[0]
    return (freq_re.reshape(CH, row_count), freq_im.reshape(CH, row_count))


def plain_shards(voltages, beam_delays, cal_gains):
    inp_dev = voltages.shape[0]
    spec_dev = voltages.shape[1] // NFFT
    tm_count = lax.axis_size("tm")
    chan_count = lax.axis_size("chan")
    spectra_total = spec_dev * tm_count
    raw_block = voltages.reshape(inp_dev, spec_dev, NFFT).transpose(1, 0, 2).astype(jnp.bfloat16)
    tail_block = shifted(raw_block[: TAPS - 1], "tm", -1)
    extended = jnp.concatenate([raw_block, tail_block], axis=0).astype(jnp.float32)
    coeffs = pfb_window()
    filtered = coeffs[0][None, None, :] * extended[0:spec_dev]
    for tap_index in range(1, TAPS):
        filtered = (
            filtered + coeffs[tap_index][None, None, :] * extended[tap_index : tap_index + spec_dev]
        )
    freq_re, freq_im = transform(filtered.reshape(spec_dev * inp_dev, FA, FB))
    packed = (jnp.stack([freq_re, freq_im]) * (1.0 / 64.0)).astype(jnp.bfloat16)
    packed = packed.reshape(2, CH, spec_dev, inp_dev)
    chan_local = CH // (tm_count * chan_count)
    reordered = packed.reshape(2, tm_count, chan_count, chan_local, spec_dev, inp_dev)
    reordered = reordered.transpose(0, 2, 1, 3, 4, 5).reshape(2, CH, spec_dev, inp_dev)
    sectioned = lax.all_to_all(reordered, "chan", split_axis=1, concat_axis=3, tiled=True)
    turned = lax.all_to_all(sectioned, "tm", split_axis=1, concat_axis=2, tiled=True)
    a_re = turned[0].astype(jnp.float32)
    a_im = turned[1].astype(jnp.float32)
    g_re = cal_gains[0][:, None, :]
    g_im = cal_gains[1][:, None, :]
    cal_re = (g_re * a_re - g_im * a_im).astype(jnp.bfloat16)
    cal_im = (g_re * a_im + g_im * a_re).astype(jnp.bfloat16)
    stacked = jnp.concatenate([cal_re, cal_im], axis=1)
    flipped = jnp.concatenate([cal_im, -cal_re], axis=1)
    vis_re = jnp.einsum("ctp,ctq->cpq", stacked, stacked, preferred_element_type=jnp.float32)
    vis_im = jnp.einsum("ctp,ctq->cpq", flipped, stacked, preferred_element_type=jnp.float32)
    visibilities = (jnp.stack([vis_re, vis_im]) / spectra_total).astype(jnp.bfloat16)
    chan_first = (
        lax.axis_index("tm") * (chan_local * chan_count) + lax.axis_index("chan") * chan_local
    )
    chan_ids = chan_first + jnp.arange(chan_local, dtype=jnp.int32)
    phase_idx = beam_delays[None, :, :] * chan_ids[:, None, None] % NFFT
    angles = phase_idx.astype(jnp.float32) * (2.0 * math.pi / NFFT)
    weight_norm = 1.0 / math.sqrt(beam_delays.shape[1])
    weight_re = (jnp.cos(angles) * weight_norm).astype(jnp.bfloat16)
    weight_im = (-jnp.sin(angles) * weight_norm).astype(jnp.bfloat16)
    beam_re = jnp.einsum(
        "cti,cbi->ctb", cal_re, weight_re, preferred_element_type=jnp.float32
    ) - jnp.einsum("cti,cbi->ctb", cal_im, weight_im, preferred_element_type=jnp.float32)
    beam_im = jnp.einsum(
        "cti,cbi->ctb", cal_im, weight_re, preferred_element_type=jnp.float32
    ) + jnp.einsum("cti,cbi->ctb", cal_re, weight_im, preferred_element_type=jnp.float32)
    beam_power = (beam_re * beam_re + beam_im * beam_im).astype(jnp.bfloat16)
    return (visibilities, beam_power)


def solution(mesh):
    return jax.shard_map(
        shards,
        mesh=mesh,
        in_specs=(P(("grp", "chan"), "tm"), P(), P(None, ("grp", "tm", "chan"), None)),
        out_specs=(
            P(None, ("grp", "tm", "chan"), None, None),
            P(("grp", "tm", "chan"), None, None),
        ),
        check_vma=False,
    )
```

```python
import functools
import math

import jax
import jax.numpy as jnp
import numpy as np
from jax import lax
from jax.experimental import pallas as pl
from jax.experimental.pallas import tpu as pltpu
from jax.sharding import PartitionSpec as P

TAPS = 4
FA = 64
FB = 64
NFFT = 4096
CH = 2048
RAD = 32
LANES = 128
PAIRS = RAD // 2
ROWS = NFFT // PAIRS
CHAN_BLOCK = 8
SLOTS = 3
AHEAD = 4
SHARES = (3, 1)
COPIES = 2
ROT = 16
MIB = 1 << 20


def shifted(block, axis, distance):
    devices = range(lax.axis_size(axis))
    route = [(i - distance, i) for i in devices if i - distance in devices]
    return lax.ppermute(block, axis, route)


def window_table():
    total_len = TAPS * NFFT
    pos = np.arange(total_len, dtype=np.float64)
    centre = (pos - total_len / 2 + 0.5) / NFFT
    taper = 0.5 - 0.5 * np.cos(2.0 * np.pi * (pos + 0.5) / total_len)
    coeffs = np.sinc(centre) * taper
    coeffs = coeffs / np.sqrt(np.sum(coeffs * coeffs))
    return coeffs.reshape(TAPS, NFFT).astype(np.float32)


def split_table(table):
    high = table.astype(jnp.bfloat16)
    low = (table - high.astype(np.float64)).astype(jnp.bfloat16)
    return high, low


def second_tables():
    lane = np.arange(LANES)
    k1 = np.arange(CH // RAD)
    table = np.zeros((PAIRS, CH // RAD, 2, 2, 2, LANES))
    for m in range(PAIRS):
        if m == 0:
            for which, k2 in enumerate((0, RAD // 2)):
                phase = (RAD * k1[:, None] + k2) * lane[None, :] % NFFT
                angle = 2.0 * np.pi * phase / NFFT
                table[m, :, which, 0, which] = np.cos(angle)
                table[m, :, which, 1, which] = -np.sin(angle)
            continue
        for which in range(2):
            channel = RAD * k1 + (m if which == 0 else RAD - m)
            source = channel if which == 0 else NFFT - channel
            sign = 1.0 if which == 0 else -1.0
            angle = 2.0 * np.pi * (source[:, None] * lane[None, :] % NFFT) / NFFT
            cos, sin = np.cos(angle), np.sin(angle)
            table[m, :, which, 0, 0] = cos
            table[m, :, which, 0, 1] = sin
            table[m, :, which, 1, 0] = -sin * sign
            table[m, :, which, 1, 1] = cos * sign
    return split_table(table.reshape(PAIRS, ROWS, 2 * LANES) / 64.0)


def real_transform(vals):
    n = len(vals)
    if n == 2:
        return [(vals[0] + vals[1], None), (vals[0] - vals[1], None)]
    even = real_transform(vals[0::2])
    odd = real_transform(vals[1::2])
    half = n // 2
    out = [None] * (half + 1)
    out[0] = (even[0][0] + odd[0][0], None)
    out[half] = (even[0][0] - odd[0][0], None)
    for k in range(1, n // 4):
        c, s = math.cos(2 * math.pi * k / n), math.sin(2 * math.pi * k / n)
        (er, ei), (sr, si) = even[k], odd[k]
        if 8 * k == n:
            tr, ti = (sr + si) * c, (si - sr) * c
        else:
            tr, ti = sr * c + si * s, si * c - sr * s
        out[k] = (er + tr, ei + ti)
        out[half - k] = (er - tr, ti - ei)
    out[n // 4] = (even[n // 4][0], -odd[n // 4][0])
    return out


def spectra_kernel(half, blocks, rows_in, steps_in, pairs, x_ref, *refs):
    halo_refs, (win_ref, high_ref, low_ref) = refs[: half + 1], refs[half + 1 : half + 4]
    out_refs, (wide, mid) = refs[-2 - len(SHARES) : -2], refs[-2:]
    step = pl.program_id(0)

    @pl.when(step < steps_in)
    def _():
        at = 0
        for ref in (x_ref, *halo_refs):
            wide[:, at : at + ref.shape[1]] = ref[...].astype(jnp.float32)
            at += ref.shape[1]
        inputs = rows_in * steps_in

        @pl.loop(0, rows_in // 8)
        def _(sub):
            rows = pl.ds(pl.multiple_of(sub * 8, 8), 8)
            for s in range(blocks):
                vals = []
                for col in range(RAD):
                    total = None
                    for tap in range(TAPS):
                        at = (s + tap) * NFFT + col * LANES
                        term = wide[rows, at : at + LANES] * win_ref[tap : tap + 1, col * LANES : (col + 1) * LANES]
                        total = term if total is None else total + term
                    vals.append(total)
                freq = real_transform(vals)
                place = pl.ds(pl.multiple_of(s * inputs + step * rows_in + sub * 8, 8), 8)
                mid[0, place, :LANES] = freq[0][0]
                mid[0, place, LANES:] = freq[PAIRS][0]
                for m in range(1, PAIRS):
                    mid[m, place, :LANES] = freq[m][0]
                    mid[m, place, LANES:] = freq[m][1]

    @pl.when(step >= steps_in)
    def _():
        first = (step - steps_in) * pairs
        owners, _, lanes = out_refs[0].shape
        unit = ROWS // owners // sum(SHARES)
        totals = []
        for p in range(pairs):
            both = mid[first + p]
            high = both.astype(jnp.bfloat16)
            low = (both - high.astype(jnp.float32)).astype(jnp.bfloat16)
            left = jnp.concatenate([high_ref[p], high_ref[p], low_ref[p]], axis=1)
            right = jnp.concatenate([high, low, high], axis=1)
            total = lax.dot_general(left, right, (((1,), (1,)), ((), ())), preferred_element_type=jnp.float32)
            totals.append(total.reshape(owners, ROWS // owners, lanes))
        start = 0
        for groups, out_ref in zip(SHARES, out_refs):
            stop = start + groups * unit
            tile = jnp.concatenate([one[:, start:stop] for one in totals], axis=1)
            out_ref[...] = tile.astype(jnp.bfloat16)
            start = stop


def spectra(half, voltages, halos, tables, owners, results):
    inputs = voltages.shape[0]
    spec = voltages.shape[1] // NFFT
    blocks = spec // 2
    lanes = inputs * blocks
    own = spec - half * blocks
    wanted = (blocks + TAPS - 1) * NFFT - own * NFFT
    rows_in, pairs = 16, 4
    steps_in, steps_out = inputs // rows_in, PAIRS // pairs
    unit = ROWS // owners // sum(SHARES)
    before = lambda g: jnp.minimum(g, steps_in - 1)
    after = lambda g: jnp.maximum(g - steps_in, 0)
    return pl.pallas_call(
        functools.partial(spectra_kernel, half, blocks, rows_in, steps_in, pairs),
        grid=(steps_in + steps_out,),
        in_specs=[pl.BlockSpec((rows_in, own * NFFT), lambda g: (before(g), half))]
        + [pl.BlockSpec((rows_in, min(wanted, halo.shape[1])), lambda g: (before(g), 0)) for halo in halos]
        + [
            pl.BlockSpec((TAPS, NFFT), lambda g: (0, 0)),
            pl.BlockSpec((pairs, ROWS, 2 * LANES), lambda g: (after(g), 0, 0)),
            pl.BlockSpec((pairs, ROWS, 2 * LANES), lambda g: (after(g), 0, 0)),
        ]
        + [pl.BlockSpec(memory_space=pl.ANY)] * len(results),
        out_specs=[pl.BlockSpec((owners, pairs * unit * n, lanes), lambda g: (0, after(g), half)) for n in SHARES],
        out_shape=[jax.ShapeDtypeStruct((owners, PAIRS * unit * n, inputs * spec), jnp.bfloat16) for n in SHARES],
        input_output_aliases={len(halos) + 4 + i: i for i in range(len(results))},
        scratch_shapes=[
            pltpu.VMEM((rows_in, (blocks + TAPS - 1) * NFFT), jnp.float32),
            pltpu.VMEM((PAIRS, lanes, 2 * LANES), jnp.float32),
        ],
        compiler_params=pltpu.CompilerParams(vmem_limit_bytes=20 * MIB),
        cost_estimate=pl.CostEstimate(flops=6 * PAIRS * ROWS * 256 * lanes, bytes_accessed=8 * MIB, transcendentals=0),
        name="spectra",
    )(voltages, *halos, *tables, *results)


def unit_circle(phase):
    quarter = NFFT // 4
    quad = (phase + quarter // 2) // quarter
    x = (phase - quad * quarter).astype(jnp.float32) * (2.0 * math.pi / NFFT)
    q = x * x
    cos = 1.0 + q * (-1 / 2 + q * (1 / 24 + q * (-1 / 720 + q * (1 / 40320))))
    sin = x * (1.0 + q * (-1 / 6 + q * (1 / 120 + q * (-1 / 5040 + q * (1 / 362880)))))
    odd = quad % 2 == 1
    c, s = jnp.where(odd, sin, cos), jnp.where(odd, cos, sin)
    c = jnp.where((quad == 1) | (quad == 2), -c, c)
    s = jnp.where((quad == 2) | (quad == 3), -s, s)
    return c, s


def weights_kernel(norm, first_ref, delay_ref, out_ref):
    delays = delay_ref[...]
    step_cos, step_sin = unit_circle(delays)

    @pl.loop(0, out_ref.shape[0] // ROT)
    def _(group):
        c, s = unit_circle(delays * (first_ref[0] + group * ROT) % NFFT)
        c, s = c * norm, s * -norm
        for j in range(ROT):
            k = group * ROT + j
            out_ref[k, 0] = c.astype(jnp.bfloat16)
            out_ref[k, 1] = s.astype(jnp.bfloat16)
            if j + 1 < ROT:
                c, s = c * step_cos + s * step_sin, s * step_cos - c * step_sin


def beam_weights(beam_delays, chan_first, chan_local):
    beams, inputs = beam_delays.shape
    rows = 16
    return pl.pallas_call(
        functools.partial(weights_kernel, 1.0 / math.sqrt(inputs)),
        grid=(inputs // rows,),
        in_specs=[
            pl.BlockSpec(memory_space=pltpu.SMEM),
            pl.BlockSpec((rows, beams), lambda g: (g, 0)),
        ],
        out_specs=pl.BlockSpec((chan_local, 2, rows, beams), lambda g: (0, 0, g, 0)),
        out_shape=jax.ShapeDtypeStruct((chan_local, 2, inputs, beams), jnp.bfloat16),
        compiler_params=pltpu.CompilerParams(vmem_limit_bytes=24 * MIB),
        cost_estimate=pl.CostEstimate(
            flops=60 * chan_local * inputs * beams, bytes_accessed=4 * chan_local * inputs * beams, transcendentals=0
        ),
        name="weights",
    )(chan_first.reshape(1), beam_delays.T)


def combine_kernel(tm_count, spec, inputs, share, out_steps, g_ref, gain_ref, w_ref, *refs):
    (vis_ref, power_ref, rows_ref, held, sems, ahead, w_sems) = refs[-7:]
    step = pl.program_id(0)
    steps = pl.num_programs(0)
    before = sum(SHARES[:share]) * (RAD // CHAN_BLOCK)
    slot = step % SLOTS

    def vis_copies(at_step):
        at = at_step % SLOTS
        wide = CHAN_BLOCK // COPIES
        for part in range(2):
            for c in range(COPIES):
                yield pltpu.make_async_copy(
                    held.at[at, part, pl.ds(c * wide, wide)],
                    vis_ref.at[part, pl.ds((before + at_step) * CHAN_BLOCK + c * wide, wide)],
                    sems.at[at, part, c],
                )

    def weight_copy(at_step):
        at = at_step % AHEAD
        return pltpu.make_async_copy(w_ref.at[pl.ds((before + at_step) * CHAN_BLOCK, CHAN_BLOCK)], ahead.at[at], w_sems.at[at])

    @pl.when(step == 0)
    def _():
        for first in range(min(AHEAD - 1, out_steps)):
            weight_copy(first).start()

    @pl.when(step + AHEAD - 1 < out_steps)
    def _():
        weight_copy(step + AHEAD - 1).start()

    @pl.when(step >= SLOTS)
    def _():
        for copy in vis_copies(step - SLOTS):
            copy.wait()

    rows = g_ref.shape[1]
    per = rows // PAIRS
    tile = 16
    times = tm_count * spec
    half = LANES // 2

    @pl.when(step == 0)
    def _():
        low_half = lax.broadcasted_iota(jnp.int32, (tile, LANES), 1) < half

        @pl.loop(0, rows // tile)
        def _(m):
            at = pl.ds(pl.multiple_of(m * tile, tile), tile)
            for t in range(tm_count):
                for pair in range(2):
                    for two in range(2):
                        cols = slice(two * LANES, (two + 1) * LANES)
                        a = g_ref[t * 4 + 2 * pair, at, cols].astype(jnp.float32)
                        b = g_ref[t * 4 + 2 * pair + 1, at, cols].astype(jnp.float32)
                        even = jnp.where(low_half, a, pltpu.roll(b, half, 1))
                        odd = jnp.where(low_half, pltpu.roll(a, half, 1), b)
                        s = t * spec + 2 * two
                        rows_ref[pair, pl.ds(pl.multiple_of(s * rows + m * tile, tile), tile), :] = even
                        rows_ref[pair, pl.ds(pl.multiple_of((s + 1) * rows + m * tile, tile), tile), :] = odd

    weight_copy(step).wait()
    scale = 1.0 / times
    blocks = RAD // CHAN_BLOCK
    for u in range(CHAN_BLOCK):
        k2 = (step % blocks) * CHAN_BLOCK + u
        upper = k2 // PAIRS
        m = jnp.where(k2 == PAIRS, 0, jnp.where(upper == 1, RAD - k2, k2))
        row = m * per + (step // blocks) * 4 + upper * 2
        z_re = jnp.concatenate([rows_ref[p, pl.ds(row, times, stride=rows), :] for p in range(2)], axis=1)
        z_im = jnp.concatenate([rows_ref[p, pl.ds(row + 1, times, stride=rows), :] for p in range(2)], axis=1)
        g_re = gain_ref[0, u : u + 1, :]
        g_im = gain_ref[1, u : u + 1, :]
        cal_re = (g_re * z_re - g_im * z_im).astype(jnp.bfloat16)
        cal_im = (g_re * z_im + g_im * z_re).astype(jnp.bfloat16)
        stacked = jnp.concatenate([cal_re, cal_im], axis=0)
        turned = jnp.concatenate([-cal_im, cal_re], axis=0)
        both = jnp.concatenate([stacked, turned], axis=1)
        vis = lax.dot_general(stacked, both, (((0,), (0,)), ((), ())), preferred_element_type=jnp.float32)
        vis = (vis * scale).astype(jnp.bfloat16)
        held[slot, 0, u] = vis[:, :inputs]
        held[slot, 1, u] = vis[:, inputs:]
        left = jnp.concatenate([stacked, turned], axis=1)
        w = ahead[step % AHEAD, u].reshape(2 * inputs, w_ref.shape[3])
        formed = lax.dot_general(left, w, (((1,), (0,)), ((), ())), preferred_element_type=jnp.float32)
        formed = formed * formed
        power_ref[u] = (formed[:times] + formed[times:]).astype(jnp.bfloat16)

    for copy in vis_copies(step):
        copy.start()

    @pl.when(step == steps - 1)
    def _():
        for back in range(min(SLOTS, out_steps) - 1, -1, -1):
            for copy in vis_copies(step - back):
                copy.wait()


def combine(gathered, cal_gains, weights, tm_count, spec, share, results):
    sources, rows, lanes = gathered.shape
    chan_local, _, inputs, beams = weights.shape
    times = tm_count * spec
    steps = SHARES[share] * (RAD // CHAN_BLOCK)
    first = sum(SHARES[:share]) * (RAD // CHAN_BLOCK)
    return pl.pallas_call(
        functools.partial(combine_kernel, tm_count, spec, inputs, share, steps),
        grid=(steps,),
        in_specs=[
            pl.BlockSpec((sources, rows, lanes), lambda g: (0, 0, 0)),
            pl.BlockSpec((2, CHAN_BLOCK, inputs), lambda g: (0, first + g, 0)),
        ]
        + [pl.BlockSpec(memory_space=pl.ANY)] * (1 + len(results)),
        input_output_aliases={3 + i: i for i in range(len(results))},
        out_specs=[
            pl.BlockSpec(memory_space=pl.ANY),
            pl.BlockSpec((CHAN_BLOCK, times, beams), lambda g: (first + g, 0, 0)),
        ],
        out_shape=[
            jax.ShapeDtypeStruct((2, chan_local, inputs, inputs), jnp.bfloat16),
            jax.ShapeDtypeStruct((chan_local, times, beams), jnp.bfloat16),
        ],
        scratch_shapes=[
            pltpu.VMEM((2, times * rows, LANES), jnp.float32),
            pltpu.VMEM((SLOTS, 2, CHAN_BLOCK, inputs, inputs), jnp.bfloat16),
            pltpu.SemaphoreType.DMA((SLOTS, 2, COPIES)),
            pltpu.VMEM((AHEAD, CHAN_BLOCK, 2, inputs, beams), jnp.bfloat16),
            pltpu.SemaphoreType.DMA((AHEAD,)),
        ],
        compiler_params=pltpu.CompilerParams(vmem_limit_bytes=28 * MIB),
        cost_estimate=pl.CostEstimate(
            flops=steps * CHAN_BLOCK * (4 * 2 * times * inputs * inputs + 8 * times * inputs * beams),
            bytes_accessed=steps * CHAN_BLOCK * (4 * inputs * inputs + 4 * inputs * beams),
            transcendentals=0,
        ),
        name="combine",
    )(gathered, cal_gains, weights, *results)


def fits(voltages, beam_delays, tm_count, chan_count):
    inp_dev, samples = voltages.shape
    spec = samples // NFFT
    owners = tm_count * chan_count
    return (
        ROWS % owners == 0
        and ROWS // owners == 16
        and CH // owners == sum(SHARES) * RAD
        and spec == 4
        and chan_count == 4
        and inp_dev * 2 == LANES
        and beam_delays.shape[1] == inp_dev * chan_count
    )


def shards(voltages, beam_delays, cal_gains):
    tm_count = lax.axis_size("tm")
    chan_count = lax.axis_size("chan")
    if not fits(voltages, beam_delays, tm_count, chan_count):
        return plain_shards(voltages, beam_delays, cal_gains)
    owners = tm_count * chan_count
    chan_local = CH // owners
    spec_dev = voltages.shape[1] // NFFT
    early = shifted(voltages[:, : 2 * NFFT].astype(jnp.bfloat16), "tm", -1)
    late = shifted(voltages[:, 2 * NFFT : (TAPS - 1) * NFFT].astype(jnp.bfloat16), "tm", -1)
    chan_first = (lax.axis_index("tm") * chan_count + lax.axis_index("chan")) * chan_local
    weights = beam_weights(beam_delays, chan_first, chan_local)
    tables = [jnp.asarray(table) for table in (window_table(), *second_tables())]
    sent = spectra(0, voltages, [early], tables, owners, ())
    sent = spectra(1, voltages, [early, late], tables, owners, sent)
    results = ()
    for share in range(len(SHARES)):
        if share:
            block, gathered, weights = lax.optimization_barrier((sent[share], gathered, weights))
            results = combine(gathered, cal_gains, weights, tm_count, spec_dev, share - 1, results)
        else:
            block = sent[share]
        gathered = lax.all_to_all(block, ("tm", "chan"), split_axis=0, concat_axis=0, tiled=True)
    visibilities, beam_power = combine(gathered, cal_gains, weights, tm_count, spec_dev, len(SHARES) - 1, results)
    return (visibilities, beam_power)


def pfb_window():
    total_len = TAPS * NFFT
    sample_pos = jnp.arange(total_len, dtype=jnp.float32)
    centre = (sample_pos - total_len / 2 + 0.5) / NFFT
    taper_win = 0.5 - 0.5 * jnp.cos(2.0 * math.pi * (sample_pos + 0.5) / total_len)
    coeffs = jnp.sinc(centre) * taper_win
    coeffs = coeffs / jnp.sqrt(jnp.sum(coeffs * coeffs))
    return coeffs.reshape(TAPS, NFFT)


def phase_table(left, right, modulus):
    phase_idx = left[:, None] * right[None, :] % modulus
    angles = phase_idx.astype(jnp.float32) * (2.0 * math.pi / modulus)
    return (jnp.cos(angles), jnp.sin(angles))


def transform(row_block):
    best = lax.Precision.HIGHEST
    first_idx = jnp.arange(FA, dtype=jnp.int32)
    second_idx = jnp.arange(FB, dtype=jnp.int32)
    half_idx = jnp.arange(FB // 2, dtype=jnp.int32)
    cos_one, sin_one = phase_table(first_idx, first_idx, FA)
    section_re = jnp.einsum("rab,ak->rkb", row_block, cos_one, precision=best)
    section_im = -jnp.einsum("rab,ak->rkb", row_block, sin_one, precision=best)
    twid_cos, twid_sin = phase_table(first_idx, second_idx, NFFT)
    inner_re = section_re * twid_cos + section_im * twid_sin
    inner_im = section_im * twid_cos - section_re * twid_sin
    cos_two, sin_two = phase_table(second_idx, half_idx, FB)
    freq_re = jnp.einsum("rkb,bq->qkr", inner_re, cos_two, precision=best) + jnp.einsum(
        "rkb,bq->qkr", inner_im, sin_two, precision=best
    )
    freq_im = jnp.einsum("rkb,bq->qkr", inner_im, cos_two, precision=best) - jnp.einsum(
        "rkb,bq->qkr", inner_re, sin_two, precision=best
    )
    row_count = row_block.shape[0]
    return (freq_re.reshape(CH, row_count), freq_im.reshape(CH, row_count))


def plain_shards(voltages, beam_delays, cal_gains):
    inp_dev = voltages.shape[0]
    spec_dev = voltages.shape[1] // NFFT
    tm_count = lax.axis_size("tm")
    chan_count = lax.axis_size("chan")
    spectra_total = spec_dev * tm_count
    raw_block = voltages.reshape(inp_dev, spec_dev, NFFT).transpose(1, 0, 2).astype(jnp.bfloat16)
    tail_block = shifted(raw_block[: TAPS - 1], "tm", -1)
    extended = jnp.concatenate([raw_block, tail_block], axis=0).astype(jnp.float32)
    coeffs = pfb_window()
    filtered = coeffs[0][None, None, :] * extended[0:spec_dev]
    for tap_index in range(1, TAPS):
        filtered = (
            filtered + coeffs[tap_index][None, None, :] * extended[tap_index : tap_index + spec_dev]
        )
    freq_re, freq_im = transform(filtered.reshape(spec_dev * inp_dev, FA, FB))
    packed = (jnp.stack([freq_re, freq_im]) * (1.0 / 64.0)).astype(jnp.bfloat16)
    packed = packed.reshape(2, CH, spec_dev, inp_dev)
    chan_local = CH // (tm_count * chan_count)
    reordered = packed.reshape(2, tm_count, chan_count, chan_local, spec_dev, inp_dev)
    reordered = reordered.transpose(0, 2, 1, 3, 4, 5).reshape(2, CH, spec_dev, inp_dev)
    sectioned = lax.all_to_all(reordered, "chan", split_axis=1, concat_axis=3, tiled=True)
    turned = lax.all_to_all(sectioned, "tm", split_axis=1, concat_axis=2, tiled=True)
    a_re = turned[0].astype(jnp.float32)
    a_im = turned[1].astype(jnp.float32)
    g_re = cal_gains[0][:, None, :]
    g_im = cal_gains[1][:, None, :]
    cal_re = (g_re * a_re - g_im * a_im).astype(jnp.bfloat16)
    cal_im = (g_re * a_im + g_im * a_re).astype(jnp.bfloat16)
    stacked = jnp.concatenate([cal_re, cal_im], axis=1)
    flipped = jnp.concatenate([cal_im, -cal_re], axis=1)
    vis_re = jnp.einsum("ctp,ctq->cpq", stacked, stacked, preferred_element_type=jnp.float32)
    vis_im = jnp.einsum("ctp,ctq->cpq", flipped, stacked, preferred_element_type=jnp.float32)
    visibilities = (jnp.stack([vis_re, vis_im]) / spectra_total).astype(jnp.bfloat16)
    chan_first = (
        lax.axis_index("tm") * (chan_local * chan_count) + lax.axis_index("chan") * chan_local
    )
    chan_ids = chan_first + jnp.arange(chan_local, dtype=jnp.int32)
    phase_idx = beam_delays[None, :, :] * chan_ids[:, None, None] % NFFT
    angles = phase_idx.astype(jnp.float32) * (2.0 * math.pi / NFFT)
    weight_norm = 1.0 / math.sqrt(beam_delays.shape[1])
    weight_re = (jnp.cos(angles) * weight_norm).astype(jnp.bfloat16)
    weight_im = (-jnp.sin(angles) * weight_norm).astype(jnp.bfloat16)
    beam_re = jnp.einsum(
        "cti,cbi->ctb", cal_re, weight_re, preferred_element_type=jnp.float32
    ) - jnp.einsum("cti,cbi->ctb", cal_im, weight_im, preferred_element_type=jnp.float32)
    beam_im = jnp.einsum(
        "cti,cbi->ctb", cal_im, weight_re, preferred_element_type=jnp.float32
    ) + jnp.einsum("cti,cbi->ctb", cal_re, weight_im, preferred_element_type=jnp.float32)
    beam_power = (beam_re * beam_re + beam_im * beam_im).astype(jnp.bfloat16)
    return (visibilities, beam_power)


def solution(mesh):
    return jax.shard_map(
        shards,
        mesh=mesh,
        in_specs=(P(("grp", "chan"), "tm"), P(), P(None, ("grp", "tm", "chan"), None)),
        out_specs=(
            P(None, ("grp", "tm", "chan"), None, None),
            P(("grp", "tm", "chan"), None, None),
        ),
        check_vma=False,
    )
```

```python
import functools
import math

import jax
import jax.numpy as jnp
import numpy as np
from jax import lax
from jax.experimental import pallas as pl
from jax.experimental.pallas import tpu as pltpu
from jax.sharding import PartitionSpec as P

TAPS = 4
FA = 64
FB = 64
NFFT = 4096
CH = 2048
RAD = 32
LANES = 128
PAIRS = RAD // 2
ROWS = NFFT // PAIRS
CHAN_BLOCK = 8
SLOTS = 3
AHEAD = 4
SHARES = (5, 3)
GROUP = RAD // 2
COPIES = 2
ROT = 16
MIB = 1 << 20


def shifted(block, axis, distance):
    devices = range(lax.axis_size(axis))
    route = [(i - distance, i) for i in devices if i - distance in devices]
    return lax.ppermute(block, axis, route)


def window_table():
    total_len = TAPS * NFFT
    pos = np.arange(total_len, dtype=np.float64)
    centre = (pos - total_len / 2 + 0.5) / NFFT
    taper = 0.5 - 0.5 * np.cos(2.0 * np.pi * (pos + 0.5) / total_len)
    coeffs = np.sinc(centre) * taper
    coeffs = coeffs / np.sqrt(np.sum(coeffs * coeffs))
    return coeffs.reshape(TAPS, NFFT).astype(np.float32)


def split_table(table):
    high = table.astype(jnp.bfloat16)
    low = (table - high.astype(np.float64)).astype(jnp.bfloat16)
    return high, low


def second_tables():
    lane = np.arange(LANES)
    k1 = np.arange(CH // RAD)
    table = np.zeros((PAIRS, CH // RAD, 2, 2, 2, LANES))
    for m in range(PAIRS):
        if m == 0:
            for which, k2 in enumerate((0, RAD // 2)):
                phase = (RAD * k1[:, None] + k2) * lane[None, :] % NFFT
                angle = 2.0 * np.pi * phase / NFFT
                table[m, :, which, 0, which] = np.cos(angle)
                table[m, :, which, 1, which] = -np.sin(angle)
            continue
        for which in range(2):
            channel = RAD * k1 + (m if which == 0 else RAD - m)
            source = channel if which == 0 else NFFT - channel
            sign = 1.0 if which == 0 else -1.0
            angle = 2.0 * np.pi * (source[:, None] * lane[None, :] % NFFT) / NFFT
            cos, sin = np.cos(angle), np.sin(angle)
            table[m, :, which, 0, 0] = cos
            table[m, :, which, 0, 1] = sin
            table[m, :, which, 1, 0] = -sin * sign
            table[m, :, which, 1, 1] = cos * sign
    return split_table(table.reshape(PAIRS, ROWS, 2 * LANES) / 64.0)


def real_transform(vals):
    n = len(vals)
    if n == 2:
        return [(vals[0] + vals[1], None), (vals[0] - vals[1], None)]
    even = real_transform(vals[0::2])
    odd = real_transform(vals[1::2])
    half = n // 2
    out = [None] * (half + 1)
    out[0] = (even[0][0] + odd[0][0], None)
    out[half] = (even[0][0] - odd[0][0], None)
    for k in range(1, n // 4):
        c, s = math.cos(2 * math.pi * k / n), math.sin(2 * math.pi * k / n)
        (er, ei), (sr, si) = even[k], odd[k]
        if 8 * k == n:
            tr, ti = (sr + si) * c, (si - sr) * c
        else:
            tr, ti = sr * c + si * s, si * c - sr * s
        out[k] = (er + tr, ei + ti)
        out[half - k] = (er - tr, ti - ei)
    out[n // 4] = (even[n // 4][0], -odd[n // 4][0])
    return out


def spectra_kernel(half, blocks, rows_in, steps_in, pairs, x_ref, *refs):
    halo_refs, (win_ref, high_ref, low_ref) = refs[: half + 1], refs[half + 1 : half + 4]
    out_refs, (wide, mid) = refs[-2 - len(SHARES) : -2], refs[-2:]
    step = pl.program_id(0)

    @pl.when(step < steps_in)
    def _():
        at = 0
        for ref in (x_ref, *halo_refs):
            wide[:, at : at + ref.shape[1]] = ref[...].astype(jnp.float32)
            at += ref.shape[1]
        inputs = rows_in * steps_in

        @pl.loop(0, rows_in // 8)
        def _(sub):
            rows = pl.ds(pl.multiple_of(sub * 8, 8), 8)
            for s in range(blocks):
                vals = []
                for col in range(RAD):
                    total = None
                    for tap in range(TAPS):
                        at = (s + tap) * NFFT + col * LANES
                        term = wide[rows, at : at + LANES] * win_ref[tap : tap + 1, col * LANES : (col + 1) * LANES]
                        total = term if total is None else total + term
                    vals.append(total)
                freq = real_transform(vals)
                place = pl.ds(pl.multiple_of(s * inputs + step * rows_in + sub * 8, 8), 8)
                mid[0, place, :LANES] = freq[0][0]
                mid[0, place, LANES:] = freq[PAIRS][0]
                for m in range(1, PAIRS):
                    mid[m, place, :LANES] = freq[m][0]
                    mid[m, place, LANES:] = freq[m][1]

    @pl.when(step >= steps_in)
    def _():
        first = (step - steps_in) * pairs
        owners, _, lanes = out_refs[0].shape
        unit = ROWS // owners // sum(SHARES)
        totals = []
        for p in range(pairs):
            both = mid[first + p]
            high = both.astype(jnp.bfloat16)
            low = (both - high.astype(jnp.float32)).astype(jnp.bfloat16)
            left = jnp.concatenate([high_ref[p], high_ref[p], low_ref[p]], axis=1)
            right = jnp.concatenate([high, low, high], axis=1)
            total = lax.dot_general(left, right, (((1,), (1,)), ((), ())), preferred_element_type=jnp.float32)
            totals.append(total.reshape(owners, ROWS // owners, lanes))
        start = 0
        for groups, out_ref in zip(SHARES, out_refs):
            stop = start + groups * unit
            tile = jnp.concatenate([one[:, start:stop] for one in totals], axis=1)
            out_ref[...] = tile.astype(jnp.bfloat16)
            start = stop


def spectra(half, voltages, halos, tables, owners, results):
    inputs = voltages.shape[0]
    spec = voltages.shape[1] // NFFT
    blocks = spec // 2
    lanes = inputs * blocks
    own = spec - half * blocks
    wanted = (blocks + TAPS - 1) * NFFT - own * NFFT
    rows_in, pairs = 16, 4
    steps_in, steps_out = inputs // rows_in, PAIRS // pairs
    unit = ROWS // owners // sum(SHARES)
    before = lambda g: jnp.minimum(g, steps_in - 1)
    after = lambda g: jnp.maximum(g - steps_in, 0)
    return pl.pallas_call(
        functools.partial(spectra_kernel, half, blocks, rows_in, steps_in, pairs),
        grid=(steps_in + steps_out,),
        in_specs=[pl.BlockSpec((rows_in, own * NFFT), lambda g: (before(g), half))]
        + [pl.BlockSpec((rows_in, min(wanted, halo.shape[1])), lambda g: (before(g), 0)) for halo in halos]
        + [
            pl.BlockSpec((TAPS, NFFT), lambda g: (0, 0)),
            pl.BlockSpec((pairs, ROWS, 2 * LANES), lambda g: (after(g), 0, 0)),
            pl.BlockSpec((pairs, ROWS, 2 * LANES), lambda g: (after(g), 0, 0)),
        ]
        + [pl.BlockSpec(memory_space=pl.ANY)] * len(results),
        out_specs=[pl.BlockSpec((owners, pairs * unit * n, lanes), lambda g: (0, after(g), half)) for n in SHARES],
        out_shape=[jax.ShapeDtypeStruct((owners, PAIRS * unit * n, inputs * spec), jnp.bfloat16) for n in SHARES],
        input_output_aliases={len(halos) + 4 + i: i for i in range(len(results))},
        scratch_shapes=[
            pltpu.VMEM((rows_in, (blocks + TAPS - 1) * NFFT), jnp.float32),
            pltpu.VMEM((PAIRS, lanes, 2 * LANES), jnp.float32),
        ],
        compiler_params=pltpu.CompilerParams(vmem_limit_bytes=20 * MIB),
        cost_estimate=pl.CostEstimate(flops=6 * PAIRS * ROWS * 256 * lanes, bytes_accessed=8 * MIB, transcendentals=0),
        name="spectra",
    )(voltages, *halos, *tables, *results)


def unit_circle(phase):
    quarter = NFFT // 4
    quad = (phase + quarter // 2) // quarter
    x = (phase - quad * quarter).astype(jnp.float32) * (2.0 * math.pi / NFFT)
    q = x * x
    cos = 1.0 + q * (-1 / 2 + q * (1 / 24 + q * (-1 / 720 + q * (1 / 40320))))
    sin = x * (1.0 + q * (-1 / 6 + q * (1 / 120 + q * (-1 / 5040 + q * (1 / 362880)))))
    odd = quad % 2 == 1
    c, s = jnp.where(odd, sin, cos), jnp.where(odd, cos, sin)
    c = jnp.where((quad == 1) | (quad == 2), -c, c)
    s = jnp.where((quad == 2) | (quad == 3), -s, s)
    return c, s


def weights_kernel(norm, first_ref, delay_ref, out_ref):
    delays = delay_ref[...]
    step_cos, step_sin = unit_circle(delays)

    @pl.loop(0, out_ref.shape[0] // ROT)
    def _(group):
        c, s = unit_circle(delays * (first_ref[0] + group * ROT) % NFFT)
        c, s = c * norm, s * -norm
        for j in range(ROT):
            k = group * ROT + j
            out_ref[k, 0] = c.astype(jnp.bfloat16)
            out_ref[k, 1] = s.astype(jnp.bfloat16)
            if j + 1 < ROT:
                c, s = c * step_cos + s * step_sin, s * step_cos - c * step_sin


def beam_weights(beam_delays, chan_first, chan_local):
    beams, inputs = beam_delays.shape
    rows = 16
    return pl.pallas_call(
        functools.partial(weights_kernel, 1.0 / math.sqrt(inputs)),
        grid=(inputs // rows,),
        in_specs=[
            pl.BlockSpec(memory_space=pltpu.SMEM),
            pl.BlockSpec((rows, beams), lambda g: (g, 0)),
        ],
        out_specs=pl.BlockSpec((chan_local, 2, rows, beams), lambda g: (0, 0, g, 0)),
        out_shape=jax.ShapeDtypeStruct((chan_local, 2, inputs, beams), jnp.bfloat16),
        compiler_params=pltpu.CompilerParams(vmem_limit_bytes=24 * MIB),
        cost_estimate=pl.CostEstimate(
            flops=60 * chan_local * inputs * beams, bytes_accessed=4 * chan_local * inputs * beams, transcendentals=0
        ),
        name="weights",
    )(chan_first.reshape(1), beam_delays.T)


def combine_kernel(tm_count, spec, inputs, share, out_steps, g_ref, gain_ref, w_ref, *refs):
    (vis_ref, power_ref, rows_ref, held, sems, ahead, w_sems) = refs[-7:]
    step = pl.program_id(0)
    steps = pl.num_programs(0)
    before = sum(SHARES[:share]) * (GROUP // CHAN_BLOCK)
    slot = step % SLOTS

    def vis_copies(at_step):
        at = at_step % SLOTS
        wide = CHAN_BLOCK // COPIES
        for part in range(2):
            for c in range(COPIES):
                yield pltpu.make_async_copy(
                    held.at[at, part, pl.ds(c * wide, wide)],
                    vis_ref.at[part, pl.ds((before + at_step) * CHAN_BLOCK + c * wide, wide)],
                    sems.at[at, part, c],
                )

    def weight_copy(at_step):
        at = at_step % AHEAD
        return pltpu.make_async_copy(w_ref.at[pl.ds((before + at_step) * CHAN_BLOCK, CHAN_BLOCK)], ahead.at[at], w_sems.at[at])

    @pl.when(step == 0)
    def _():
        for first in range(min(AHEAD - 1, out_steps)):
            weight_copy(first).start()

    @pl.when(step + AHEAD - 1 < out_steps)
    def _():
        weight_copy(step + AHEAD - 1).start()

    @pl.when(step >= SLOTS)
    def _():
        for copy in vis_copies(step - SLOTS):
            copy.wait()

    rows = g_ref.shape[1]
    per = rows // PAIRS
    tile = 16
    times = tm_count * spec
    half = LANES // 2

    @pl.when(step == 0)
    def _():
        low_half = lax.broadcasted_iota(jnp.int32, (tile, LANES), 1) < half

        @pl.loop(0, rows // tile)
        def _(m):
            at = pl.ds(pl.multiple_of(m * tile, tile), tile)
            for t in range(tm_count):
                for pair in range(2):
                    for two in range(2):
                        cols = slice(two * LANES, (two + 1) * LANES)
                        a = g_ref[t * 4 + 2 * pair, at, cols].astype(jnp.float32)
                        b = g_ref[t * 4 + 2 * pair + 1, at, cols].astype(jnp.float32)
                        even = jnp.where(low_half, a, pltpu.roll(b, half, 1))
                        odd = jnp.where(low_half, pltpu.roll(a, half, 1), b)
                        s = t * spec + 2 * two
                        rows_ref[pair, pl.ds(pl.multiple_of(s * rows + m * tile, tile), tile), :] = even
                        rows_ref[pair, pl.ds(pl.multiple_of((s + 1) * rows + m * tile, tile), tile), :] = odd

    weight_copy(step).wait()
    scale = 1.0 / times
    blocks = RAD // CHAN_BLOCK
    for u in range(CHAN_BLOCK):
        k2 = ((before + step) % blocks) * CHAN_BLOCK + u
        upper = k2 // PAIRS
        m = jnp.where(k2 == PAIRS, 0, jnp.where(upper == 1, RAD - k2, k2))
        row = m * per + ((before + step) // blocks) * 4 + upper * 2 - 2 * sum(SHARES[:share])
        z_re = jnp.concatenate([rows_ref[p, pl.ds(row, times, stride=rows), :] for p in range(2)], axis=1)
        z_im = jnp.concatenate([rows_ref[p, pl.ds(row + 1, times, stride=rows), :] for p in range(2)], axis=1)
        g_re = gain_ref[0, u : u + 1, :]
        g_im = gain_ref[1, u : u + 1, :]
        cal_re = (g_re * z_re - g_im * z_im).astype(jnp.bfloat16)
        cal_im = (g_re * z_im + g_im * z_re).astype(jnp.bfloat16)
        stacked = jnp.concatenate([cal_re, cal_im], axis=0)
        turned = jnp.concatenate([-cal_im, cal_re], axis=0)
        both = jnp.concatenate([stacked, turned], axis=1)
        vis = lax.dot_general(stacked, both, (((0,), (0,)), ((), ())), preferred_element_type=jnp.float32)
        vis = (vis * scale).astype(jnp.bfloat16)
        held[slot, 0, u] = vis[:, :inputs]
        held[slot, 1, u] = vis[:, inputs:]
        left = jnp.concatenate([stacked, turned], axis=1)
        w = ahead[step % AHEAD, u].reshape(2 * inputs, w_ref.shape[3])
        formed = lax.dot_general(left, w, (((1,), (0,)), ((), ())), preferred_element_type=jnp.float32)
        formed = formed * formed
        power_ref[u] = (formed[:times] + formed[times:]).astype(jnp.bfloat16)

    for copy in vis_copies(step):
        copy.start()

    @pl.when(step == steps - 1)
    def _():
        for back in range(min(SLOTS, out_steps) - 1, -1, -1):
            for copy in vis_copies(step - back):
                copy.wait()


def combine(gathered, cal_gains, weights, tm_count, spec, share, results):
    sources, rows, lanes = gathered.shape
    chan_local, _, inputs, beams = weights.shape
    times = tm_count * spec
    steps = SHARES[share] * (GROUP // CHAN_BLOCK)
    first = sum(SHARES[:share]) * (GROUP // CHAN_BLOCK)
    return pl.pallas_call(
        functools.partial(combine_kernel, tm_count, spec, inputs, share, steps),
        grid=(steps,),
        in_specs=[
            pl.BlockSpec((sources, rows, lanes), lambda g: (0, 0, 0)),
            pl.BlockSpec((2, CHAN_BLOCK, inputs), lambda g: (0, first + g, 0)),
        ]
        + [pl.BlockSpec(memory_space=pl.ANY)] * (1 + len(results)),
        input_output_aliases={3 + i: i for i in range(len(results))},
        out_specs=[
            pl.BlockSpec(memory_space=pl.ANY),
            pl.BlockSpec((CHAN_BLOCK, times, beams), lambda g: (first + g, 0, 0)),
        ],
        out_shape=[
            jax.ShapeDtypeStruct((2, chan_local, inputs, inputs), jnp.bfloat16),
            jax.ShapeDtypeStruct((chan_local, times, beams), jnp.bfloat16),
        ],
        scratch_shapes=[
            pltpu.VMEM((2, times * rows, LANES), jnp.float32),
            pltpu.VMEM((SLOTS, 2, CHAN_BLOCK, inputs, inputs), jnp.bfloat16),
            pltpu.SemaphoreType.DMA((SLOTS, 2, COPIES)),
            pltpu.VMEM((AHEAD, CHAN_BLOCK, 2, inputs, beams), jnp.bfloat16),
            pltpu.SemaphoreType.DMA((AHEAD,)),
        ],
        compiler_params=pltpu.CompilerParams(vmem_limit_bytes=28 * MIB),
        cost_estimate=pl.CostEstimate(
            flops=steps * CHAN_BLOCK * (4 * 2 * times * inputs * inputs + 8 * times * inputs * beams),
            bytes_accessed=steps * CHAN_BLOCK * (4 * inputs * inputs + 4 * inputs * beams),
            transcendentals=0,
        ),
        name="combine",
    )(gathered, cal_gains, weights, *results)


def fits(voltages, beam_delays, tm_count, chan_count):
    inp_dev, samples = voltages.shape
    spec = samples // NFFT
    owners = tm_count * chan_count
    return (
        ROWS % owners == 0
        and ROWS // owners == 16
        and CH // owners == sum(SHARES) * GROUP
        and spec == 4
        and chan_count == 4
        and inp_dev * 2 == LANES
        and beam_delays.shape[1] == inp_dev * chan_count
    )


def shards(voltages, beam_delays, cal_gains):
    tm_count = lax.axis_size("tm")
    chan_count = lax.axis_size("chan")
    if not fits(voltages, beam_delays, tm_count, chan_count):
        return plain_shards(voltages, beam_delays, cal_gains)
    owners = tm_count * chan_count
    chan_local = CH // owners
    spec_dev = voltages.shape[1] // NFFT
    early = shifted(voltages[:, : 2 * NFFT].astype(jnp.bfloat16), "tm", -1)
    late = shifted(voltages[:, 2 * NFFT : (TAPS - 1) * NFFT].astype(jnp.bfloat16), "tm", -1)
    chan_first = (lax.axis_index("tm") * chan_count + lax.axis_index("chan")) * chan_local
    weights = beam_weights(beam_delays, chan_first, chan_local)
    tables = [jnp.asarray(table) for table in (window_table(), *second_tables())]
    sent = spectra(0, voltages, [early], tables, owners, ())
    sent = spectra(1, voltages, [early, late], tables, owners, sent)
    results = ()
    for share in range(len(SHARES)):
        if share:
            block, gathered, weights = lax.optimization_barrier((sent[share], gathered, weights))
            results = combine(gathered, cal_gains, weights, tm_count, spec_dev, share - 1, results)
        else:
            block = sent[share]
        gathered = lax.all_to_all(block, ("tm", "chan"), split_axis=0, concat_axis=0, tiled=True)
    visibilities, beam_power = combine(gathered, cal_gains, weights, tm_count, spec_dev, len(SHARES) - 1, results)
    return (visibilities, beam_power)


def pfb_window():
    total_len = TAPS * NFFT
    sample_pos = jnp.arange(total_len, dtype=jnp.float32)
    centre = (sample_pos - total_len / 2 + 0.5) / NFFT
    taper_win = 0.5 - 0.5 * jnp.cos(2.0 * math.pi * (sample_pos + 0.5) / total_len)
    coeffs = jnp.sinc(centre) * taper_win
    coeffs = coeffs / jnp.sqrt(jnp.sum(coeffs * coeffs))
    return coeffs.reshape(TAPS, NFFT)


def phase_table(left, right, modulus):
    phase_idx = left[:, None] * right[None, :] % modulus
    angles = phase_idx.astype(jnp.float32) * (2.0 * math.pi / modulus)
    return (jnp.cos(angles), jnp.sin(angles))


def transform(row_block):
    best = lax.Precision.HIGHEST
    first_idx = jnp.arange(FA, dtype=jnp.int32)
    second_idx = jnp.arange(FB, dtype=jnp.int32)
    half_idx = jnp.arange(FB // 2, dtype=jnp.int32)
    cos_one, sin_one = phase_table(first_idx, first_idx, FA)
    section_re = jnp.einsum("rab,ak->rkb", row_block, cos_one, precision=best)
    section_im = -jnp.einsum("rab,ak->rkb", row_block, sin_one, precision=best)
    twid_cos, twid_sin = phase_table(first_idx, second_idx, NFFT)
    inner_re = section_re * twid_cos + section_im * twid_sin
    inner_im = section_im * twid_cos - section_re * twid_sin
    cos_two, sin_two = phase_table(second_idx, half_idx, FB)
    freq_re = jnp.einsum("rkb,bq->qkr", inner_re, cos_two, precision=best) + jnp.einsum(
        "rkb,bq->qkr", inner_im, sin_two, precision=best
    )
    freq_im = jnp.einsum("rkb,bq->qkr", inner_im, cos_two, precision=best) - jnp.einsum(
        "rkb,bq->qkr", inner_re, sin_two, precision=best
    )
    row_count = row_block.shape[0]
    return (freq_re.reshape(CH, row_count), freq_im.reshape(CH, row_count))


def plain_shards(voltages, beam_delays, cal_gains):
    inp_dev = voltages.shape[0]
    spec_dev = voltages.shape[1] // NFFT
    tm_count = lax.axis_size("tm")
    chan_count = lax.axis_size("chan")
    spectra_total = spec_dev * tm_count
    raw_block = voltages.reshape(inp_dev, spec_dev, NFFT).transpose(1, 0, 2).astype(jnp.bfloat16)
    tail_block = shifted(raw_block[: TAPS - 1], "tm", -1)
    extended = jnp.concatenate([raw_block, tail_block], axis=0).astype(jnp.float32)
    coeffs = pfb_window()
    filtered = coeffs[0][None, None, :] * extended[0:spec_dev]
    for tap_index in range(1, TAPS):
        filtered = (
            filtered + coeffs[tap_index][None, None, :] * extended[tap_index : tap_index + spec_dev]
        )
    freq_re, freq_im = transform(filtered.reshape(spec_dev * inp_dev, FA, FB))
    packed = (jnp.stack([freq_re, freq_im]) * (1.0 / 64.0)).astype(jnp.bfloat16)
    packed = packed.reshape(2, CH, spec_dev, inp_dev)
    chan_local = CH // (tm_count * chan_count)
    reordered = packed.reshape(2, tm_count, chan_count, chan_local, spec_dev, inp_dev)
    reordered = reordered.transpose(0, 2, 1, 3, 4, 5).reshape(2, CH, spec_dev, inp_dev)
    sectioned = lax.all_to_all(reordered, "chan", split_axis=1, concat_axis=3, tiled=True)
    turned = lax.all_to_all(sectioned, "tm", split_axis=1, concat_axis=2, tiled=True)
    a_re = turned[0].astype(jnp.float32)
    a_im = turned[1].astype(jnp.float32)
    g_re = cal_gains[0][:, None, :]
    g_im = cal_gains[1][:, None, :]
    cal_re = (g_re * a_re - g_im * a_im).astype(jnp.bfloat16)
    cal_im = (g_re * a_im + g_im * a_re).astype(jnp.bfloat16)
    stacked = jnp.concatenate([cal_re, cal_im], axis=1)
    flipped = jnp.concatenate([cal_im, -cal_re], axis=1)
    vis_re = jnp.einsum("ctp,ctq->cpq", stacked, stacked, preferred_element_type=jnp.float32)
    vis_im = jnp.einsum("ctp,ctq->cpq", flipped, stacked, preferred_element_type=jnp.float32)
    visibilities = (jnp.stack([vis_re, vis_im]) / spectra_total).astype(jnp.bfloat16)
    chan_first = (
        lax.axis_index("tm") * (chan_local * chan_count) + lax.axis_index("chan") * chan_local
    )
    chan_ids = chan_first + jnp.arange(chan_local, dtype=jnp.int32)
    phase_idx = beam_delays[None, :, :] * chan_ids[:, None, None] % NFFT
    angles = phase_idx.astype(jnp.float32) * (2.0 * math.pi / NFFT)
    weight_norm = 1.0 / math.sqrt(beam_delays.shape[1])
    weight_re = (jnp.cos(angles) * weight_norm).astype(jnp.bfloat16)
    weight_im = (-jnp.sin(angles) * weight_norm).astype(jnp.bfloat16)
    beam_re = jnp.einsum(
        "cti,cbi->ctb", cal_re, weight_re, preferred_element_type=jnp.float32
    ) - jnp.einsum("cti,cbi->ctb", cal_im, weight_im, preferred_element_type=jnp.float32)
    beam_im = jnp.einsum(
        "cti,cbi->ctb", cal_im, weight_re, preferred_element_type=jnp.float32
    ) + jnp.einsum("cti,cbi->ctb", cal_re, weight_im, preferred_element_type=jnp.float32)
    beam_power = (beam_re * beam_re + beam_im * beam_im).astype(jnp.bfloat16)
    return (visibilities, beam_power)


def solution(mesh):
    return jax.shard_map(
        shards,
        mesh=mesh,
        in_specs=(P(("grp", "chan"), "tm"), P(), P(None, ("grp", "tm", "chan"), None)),
        out_specs=(
            P(None, ("grp", "tm", "chan"), None, None),
            P(("grp", "tm", "chan"), None, None),
        ),
        check_vma=False,
    )
```

```python
import functools
import math

import jax
import jax.numpy as jnp
import numpy as np
from jax import lax
from jax.experimental import pallas as pl
from jax.experimental.pallas import tpu as pltpu
from jax.sharding import PartitionSpec as P

TAPS = 4
FA = 64
FB = 64
NFFT = 4096
CH = 2048
RAD = 32
LANES = 128
PAIRS = RAD // 2
ROWS = NFFT // PAIRS
CHAN_BLOCK = 8
SLOTS = 3
AHEAD = 4
SHARES = (5, 3)
GROUP = RAD // 2
COPIES = 2
ROT = 16
MIB = 1 << 20


def shifted(block, axis, distance):
    devices = range(lax.axis_size(axis))
    route = [(i - distance, i) for i in devices if i - distance in devices]
    return lax.ppermute(block, axis, route)


def window_table():
    total_len = TAPS * NFFT
    pos = np.arange(total_len, dtype=np.float64)
    centre = (pos - total_len / 2 + 0.5) / NFFT
    taper = 0.5 - 0.5 * np.cos(2.0 * np.pi * (pos + 0.5) / total_len)
    coeffs = np.sinc(centre) * taper
    coeffs = coeffs / np.sqrt(np.sum(coeffs * coeffs))
    return coeffs.reshape(TAPS, NFFT).astype(np.float32)


def split_table(table):
    high = table.astype(jnp.bfloat16)
    low = (table - high.astype(np.float64)).astype(jnp.bfloat16)
    return high, low


def second_tables():
    lane = np.arange(LANES)
    k1 = np.arange(CH // RAD)
    table = np.zeros((PAIRS, CH // RAD, 2, 2, 2, LANES))
    for m in range(PAIRS):
        if m == 0:
            for which, k2 in enumerate((0, RAD // 2)):
                phase = (RAD * k1[:, None] + k2) * lane[None, :] % NFFT
                angle = 2.0 * np.pi * phase / NFFT
                table[m, :, which, 0, which] = np.cos(angle)
                table[m, :, which, 1, which] = -np.sin(angle)
            continue
        for which in range(2):
            channel = RAD * k1 + (m if which == 0 else RAD - m)
            source = channel if which == 0 else NFFT - channel
            sign = 1.0 if which == 0 else -1.0
            angle = 2.0 * np.pi * (source[:, None] * lane[None, :] % NFFT) / NFFT
            cos, sin = np.cos(angle), np.sin(angle)
            table[m, :, which, 0, 0] = cos
            table[m, :, which, 0, 1] = sin
            table[m, :, which, 1, 0] = -sin * sign
            table[m, :, which, 1, 1] = cos * sign
    return split_table(table.reshape(PAIRS, ROWS, 2 * LANES) / 64.0)


def real_transform(vals):
    n = len(vals)
    if n == 2:
        return [(vals[0] + vals[1], None), (vals[0] - vals[1], None)]
    even = real_transform(vals[0::2])
    odd = real_transform(vals[1::2])
    half = n // 2
    out = [None] * (half + 1)
    out[0] = (even[0][0] + odd[0][0], None)
    out[half] = (even[0][0] - odd[0][0], None)
    for k in range(1, n // 4):
        c, s = math.cos(2 * math.pi * k / n), math.sin(2 * math.pi * k / n)
        (er, ei), (sr, si) = even[k], odd[k]
        if 8 * k == n:
            tr, ti = (sr + si) * c, (si - sr) * c
        else:
            tr, ti = sr * c + si * s, si * c - sr * s
        out[k] = (er + tr, ei + ti)
        out[half - k] = (er - tr, ti - ei)
    out[n // 4] = (even[n // 4][0], -odd[n // 4][0])
    return out


def spectra_kernel(half, blocks, rows_in, steps_in, pairs, x_ref, *refs):
    halo_refs, (win_ref, high_ref, low_ref) = refs[: half + 1], refs[half + 1 : half + 4]
    out_refs, (wide, mid) = refs[-2 - len(SHARES) : -2], refs[-2:]
    step = pl.program_id(0)

    @pl.when(step < steps_in)
    def _():
        at = 0
        for ref in (x_ref, *halo_refs):
            wide[:, at : at + ref.shape[1]] = ref[...].astype(jnp.float32)
            at += ref.shape[1]
        inputs = rows_in * steps_in

        @pl.loop(0, rows_in // 8)
        def _(sub):
            rows = pl.ds(pl.multiple_of(sub * 8, 8), 8)
            for s in range(blocks):
                vals = []
                for col in range(RAD):
                    total = None
                    for tap in range(TAPS):
                        at = (s + tap) * NFFT + col * LANES
                        term = wide[rows, at : at + LANES] * win_ref[tap : tap + 1, col * LANES : (col + 1) * LANES]
                        total = term if total is None else total + term
                    vals.append(total)
                freq = real_transform(vals)
                place = pl.ds(pl.multiple_of(s * inputs + step * rows_in + sub * 8, 8), 8)
                mid[0, place, :LANES] = freq[0][0]
                mid[0, place, LANES:] = freq[PAIRS][0]
                for m in range(1, PAIRS):
                    mid[m, place, :LANES] = freq[m][0]
                    mid[m, place, LANES:] = freq[m][1]

    @pl.when(step >= steps_in)
    def _():
        first = (step - steps_in) * pairs
        owners, _, lanes = out_refs[0].shape
        unit = ROWS // owners // sum(SHARES)
        totals = []
        for p in range(pairs):
            both = mid[first + p]
            high = both.astype(jnp.bfloat16)
            low = (both - high.astype(jnp.float32)).astype(jnp.bfloat16)
            left = jnp.concatenate([high_ref[p], high_ref[p], low_ref[p]], axis=1)
            right = jnp.concatenate([high, low, high], axis=1)
            total = lax.dot_general(left, right, (((1,), (1,)), ((), ())), preferred_element_type=jnp.float32)
            totals.append(total.reshape(owners, ROWS // owners, lanes))
        start = 0
        for groups, out_ref in zip(SHARES, out_refs):
            stop = start + groups * unit
            tile = jnp.concatenate([one[:, start:stop] for one in totals], axis=1)
            out_ref[...] = tile.astype(jnp.bfloat16)
            start = stop


def spectra(half, voltages, halos, tables, owners, results):
    inputs = voltages.shape[0]
    spec = voltages.shape[1] // NFFT
    blocks = spec // 2
    lanes = inputs * blocks
    own = spec - half * blocks
    wanted = (blocks + TAPS - 1) * NFFT - own * NFFT
    rows_in, pairs = 32, 8
    steps_in, steps_out = inputs // rows_in, PAIRS // pairs
    unit = ROWS // owners // sum(SHARES)
    before = lambda g: jnp.minimum(g, steps_in - 1)
    after = lambda g: jnp.maximum(g - steps_in, 0)
    return pl.pallas_call(
        functools.partial(spectra_kernel, half, blocks, rows_in, steps_in, pairs),
        grid=(steps_in + steps_out,),
        in_specs=[pl.BlockSpec((rows_in, own * NFFT), lambda g: (before(g), half))]
        + [pl.BlockSpec((rows_in, min(wanted, halo.shape[1])), lambda g: (before(g), 0)) for halo in halos]
        + [
            pl.BlockSpec((TAPS, NFFT), lambda g: (0, 0)),
            pl.BlockSpec((pairs, ROWS, 2 * LANES), lambda g: (after(g), 0, 0)),
            pl.BlockSpec((pairs, ROWS, 2 * LANES), lambda g: (after(g), 0, 0)),
        ]
        + [pl.BlockSpec(memory_space=pl.ANY)] * len(results),
        out_specs=[pl.BlockSpec((owners, pairs * unit * n, lanes), lambda g: (0, after(g), half)) for n in SHARES],
        out_shape=[jax.ShapeDtypeStruct((owners, PAIRS * unit * n, inputs * spec), jnp.bfloat16) for n in SHARES],
        input_output_aliases={len(halos) + 4 + i: i for i in range(len(results))},
        scratch_shapes=[
            pltpu.VMEM((rows_in, (blocks + TAPS - 1) * NFFT), jnp.float32),
            pltpu.VMEM((PAIRS, lanes, 2 * LANES), jnp.float32),
        ],
        compiler_params=pltpu.CompilerParams(vmem_limit_bytes=20 * MIB),
        cost_estimate=pl.CostEstimate(flops=6 * PAIRS * ROWS * 256 * lanes, bytes_accessed=8 * MIB, transcendentals=0),
        name="spectra",
    )(voltages, *halos, *tables, *results)


def unit_circle(phase):
    quarter = NFFT // 4
    quad = (phase + quarter // 2) // quarter
    x = (phase - quad * quarter).astype(jnp.float32) * (2.0 * math.pi / NFFT)
    q = x * x
    cos = 1.0 + q * (-1 / 2 + q * (1 / 24 + q * (-1 / 720 + q * (1 / 40320))))
    sin = x * (1.0 + q * (-1 / 6 + q * (1 / 120 + q * (-1 / 5040 + q * (1 / 362880)))))
    odd = quad % 2 == 1
    c, s = jnp.where(odd, sin, cos), jnp.where(odd, cos, sin)
    c = jnp.where((quad == 1) | (quad == 2), -c, c)
    s = jnp.where((quad == 2) | (quad == 3), -s, s)
    return c, s


def weights_kernel(norm, first_ref, delay_ref, out_ref):
    delays = delay_ref[...]
    step_cos, step_sin = unit_circle(delays)

    @pl.loop(0, out_ref.shape[0] // ROT)
    def _(group):
        c, s = unit_circle(delays * (first_ref[0] + group * ROT) % NFFT)
        c, s = c * norm, s * -norm
        for j in range(ROT):
            k = group * ROT + j
            out_ref[k, 0] = c.astype(jnp.bfloat16)
            out_ref[k, 1] = s.astype(jnp.bfloat16)
            if j + 1 < ROT:
                c, s = c * step_cos + s * step_sin, s * step_cos - c * step_sin


def beam_weights(beam_delays, chan_first, chan_local):
    beams, inputs = beam_delays.shape
    rows = 16
    return pl.pallas_call(
        functools.partial(weights_kernel, 1.0 / math.sqrt(inputs)),
        grid=(inputs // rows,),
        in_specs=[
            pl.BlockSpec(memory_space=pltpu.SMEM),
            pl.BlockSpec((rows, beams), lambda g: (g, 0)),
        ],
        out_specs=pl.BlockSpec((chan_local, 2, rows, beams), lambda g: (0, 0, g, 0)),
        out_shape=jax.ShapeDtypeStruct((chan_local, 2, inputs, beams), jnp.bfloat16),
        compiler_params=pltpu.CompilerParams(vmem_limit_bytes=24 * MIB),
        cost_estimate=pl.CostEstimate(
            flops=60 * chan_local * inputs * beams, bytes_accessed=4 * chan_local * inputs * beams, transcendentals=0
        ),
        name="weights",
    )(chan_first.reshape(1), beam_delays.T)


def combine_kernel(tm_count, spec, inputs, share, out_steps, g_ref, gain_ref, w_ref, *refs):
    (vis_ref, power_ref, rows_ref, held, sems, ahead, w_sems) = refs[-7:]
    step = pl.program_id(0)
    steps = pl.num_programs(0)
    before = sum(SHARES[:share]) * (GROUP // CHAN_BLOCK)
    slot = step % SLOTS

    def vis_copies(at_step, pieces=range(COPIES)):
        at = at_step % SLOTS
        wide = CHAN_BLOCK // COPIES
        for part in range(2):
            for c in pieces:
                yield pltpu.make_async_copy(
                    held.at[at, part, pl.ds(c * wide, wide)],
                    vis_ref.at[part, pl.ds((before + at_step) * CHAN_BLOCK + c * wide, wide)],
                    sems.at[at, part, c],
                )

    def weight_copy(at_step):
        at = at_step % AHEAD
        return pltpu.make_async_copy(w_ref.at[pl.ds((before + at_step) * CHAN_BLOCK, CHAN_BLOCK)], ahead.at[at], w_sems.at[at])

    @pl.when(step == 0)
    def _():
        for first in range(min(AHEAD - 1, out_steps)):
            weight_copy(first).start()

    @pl.when(step + AHEAD - 1 < out_steps)
    def _():
        weight_copy(step + AHEAD - 1).start()

    @pl.when(step >= SLOTS)
    def _():
        for copy in vis_copies(step - SLOTS):
            copy.wait()

    rows = g_ref.shape[1]
    per = rows // PAIRS
    tile = 16
    times = tm_count * spec
    half = LANES // 2

    @pl.when(step == 0)
    def _():
        low_half = lax.broadcasted_iota(jnp.int32, (tile, LANES), 1) < half

        @pl.loop(0, rows // tile)
        def _(m):
            at = pl.ds(pl.multiple_of(m * tile, tile), tile)
            for t in range(tm_count):
                for pair in range(2):
                    for two in range(2):
                        cols = slice(two * LANES, (two + 1) * LANES)
                        a = g_ref[t * 4 + 2 * pair, at, cols].astype(jnp.float32)
                        b = g_ref[t * 4 + 2 * pair + 1, at, cols].astype(jnp.float32)
                        even = jnp.where(low_half, a, pltpu.roll(b, half, 1))
                        odd = jnp.where(low_half, pltpu.roll(a, half, 1), b)
                        s = t * spec + 2 * two
                        rows_ref[pair, pl.ds(pl.multiple_of(s * rows + m * tile, tile), tile), :] = even
                        rows_ref[pair, pl.ds(pl.multiple_of((s + 1) * rows + m * tile, tile), tile), :] = odd

    weight_copy(step).wait()
    scale = 1.0 / times
    blocks = RAD // CHAN_BLOCK
    for u in range(CHAN_BLOCK):
        k2 = ((before + step) % blocks) * CHAN_BLOCK + u
        upper = k2 // PAIRS
        m = jnp.where(k2 == PAIRS, 0, jnp.where(upper == 1, RAD - k2, k2))
        row = m * per + ((before + step) // blocks) * 4 + upper * 2 - 2 * sum(SHARES[:share])
        z_re = jnp.concatenate([rows_ref[p, pl.ds(row, times, stride=rows), :] for p in range(2)], axis=1)
        z_im = jnp.concatenate([rows_ref[p, pl.ds(row + 1, times, stride=rows), :] for p in range(2)], axis=1)
        g_re = gain_ref[0, u : u + 1, :]
        g_im = gain_ref[1, u : u + 1, :]
        cal_re = (g_re * z_re - g_im * z_im).astype(jnp.bfloat16)
        cal_im = (g_re * z_im + g_im * z_re).astype(jnp.bfloat16)
        stacked = jnp.concatenate([cal_re, cal_im], axis=0)
        turned = jnp.concatenate([-cal_im, cal_re], axis=0)
        both = jnp.concatenate([stacked, turned], axis=1)
        vis = lax.dot_general(stacked, both, (((0,), (0,)), ((), ())), preferred_element_type=jnp.float32)
        vis = (vis * scale).astype(jnp.bfloat16)
        held[slot, 0, u] = vis[:, :inputs]
        held[slot, 1, u] = vis[:, inputs:]
        left = jnp.concatenate([stacked, turned], axis=1)
        w = ahead[step % AHEAD, u].reshape(2 * inputs, w_ref.shape[3])
        formed = lax.dot_general(left, w, (((1,), (0,)), ((), ())), preferred_element_type=jnp.float32)
        formed = formed * formed
        power_ref[u] = (formed[:times] + formed[times:]).astype(jnp.bfloat16)
        if (u + 1) % (CHAN_BLOCK // COPIES) == 0:
            for copy in vis_copies(step, [u // (CHAN_BLOCK // COPIES)]):
                copy.start()


    @pl.when(step == steps - 1)
    def _():
        for back in range(min(SLOTS, out_steps) - 1, -1, -1):
            for copy in vis_copies(step - back):
                copy.wait()


def combine(gathered, cal_gains, weights, tm_count, spec, share, results):
    sources, rows, lanes = gathered.shape
    chan_local, _, inputs, beams = weights.shape
    times = tm_count * spec
    steps = SHARES[share] * (GROUP // CHAN_BLOCK)
    first = sum(SHARES[:share]) * (GROUP // CHAN_BLOCK)
    return pl.pallas_call(
        functools.partial(combine_kernel, tm_count, spec, inputs, share, steps),
        grid=(steps,),
        in_specs=[
            pl.BlockSpec((sources, rows, lanes), lambda g: (0, 0, 0)),
            pl.BlockSpec((2, CHAN_BLOCK, inputs), lambda g: (0, first + g, 0)),
        ]
        + [pl.BlockSpec(memory_space=pl.ANY)] * (1 + len(results)),
        input_output_aliases={3 + i: i for i in range(len(results))},
        out_specs=[
            pl.BlockSpec(memory_space=pl.ANY),
            pl.BlockSpec((CHAN_BLOCK, times, beams), lambda g: (first + g, 0, 0)),
        ],
        out_shape=[
            jax.ShapeDtypeStruct((2, chan_local, inputs, inputs), jnp.bfloat16),
            jax.ShapeDtypeStruct((chan_local, times, beams), jnp.bfloat16),
        ],
        scratch_shapes=[
            pltpu.VMEM((2, times * rows, LANES), jnp.float32),
            pltpu.VMEM((SLOTS, 2, CHAN_BLOCK, inputs, inputs), jnp.bfloat16),
            pltpu.SemaphoreType.DMA((SLOTS, 2, COPIES)),
            pltpu.VMEM((AHEAD, CHAN_BLOCK, 2, inputs, beams), jnp.bfloat16),
            pltpu.SemaphoreType.DMA((AHEAD,)),
        ],
        compiler_params=pltpu.CompilerParams(vmem_limit_bytes=28 * MIB),
        cost_estimate=pl.CostEstimate(
            flops=steps * CHAN_BLOCK * (4 * 2 * times * inputs * inputs + 8 * times * inputs * beams),
            bytes_accessed=steps * CHAN_BLOCK * (4 * inputs * inputs + 4 * inputs * beams),
            transcendentals=0,
        ),
        name="combine",
    )(gathered, cal_gains, weights, *results)


def fits(voltages, beam_delays, tm_count, chan_count):
    inp_dev, samples = voltages.shape
    spec = samples // NFFT
    owners = tm_count * chan_count
    return (
        ROWS % owners == 0
        and ROWS // owners == 16
        and CH // owners == sum(SHARES) * GROUP
        and spec == 4
        and chan_count == 4
        and inp_dev * 2 == LANES
        and beam_delays.shape[1] == inp_dev * chan_count
    )


def shards(voltages, beam_delays, cal_gains):
    tm_count = lax.axis_size("tm")
    chan_count = lax.axis_size("chan")
    if not fits(voltages, beam_delays, tm_count, chan_count):
        return plain_shards(voltages, beam_delays, cal_gains)
    owners = tm_count * chan_count
    chan_local = CH // owners
    spec_dev = voltages.shape[1] // NFFT
    head = lax.optimization_barrier(voltages[:, : (TAPS - 1) * NFFT].astype(jnp.bfloat16))
    early = shifted(head[:, : 2 * NFFT], "tm", -1)
    late = shifted(head[:, 2 * NFFT :], "tm", -1)
    chan_first = (lax.axis_index("tm") * chan_count + lax.axis_index("chan")) * chan_local
    weights = beam_weights(beam_delays, chan_first, chan_local)
    tables = [jnp.asarray(table) for table in (window_table(), *second_tables())]
    sent = spectra(0, voltages, [early], tables, owners, ())
    sent = spectra(1, voltages, [early, late], tables, owners, sent)
    results = ()
    for share in range(len(SHARES)):
        if share:
            block, gathered, weights = lax.optimization_barrier((sent[share], gathered, weights))
            results = combine(gathered, cal_gains, weights, tm_count, spec_dev, share - 1, results)
        else:
            block = sent[share]
        gathered = lax.all_to_all(block, ("tm", "chan"), split_axis=0, concat_axis=0, tiled=True)
    visibilities, beam_power = combine(gathered, cal_gains, weights, tm_count, spec_dev, len(SHARES) - 1, results)
    return (visibilities, beam_power)


def pfb_window():
    total_len = TAPS * NFFT
    sample_pos = jnp.arange(total_len, dtype=jnp.float32)
    centre = (sample_pos - total_len / 2 + 0.5) / NFFT
    taper_win = 0.5 - 0.5 * jnp.cos(2.0 * math.pi * (sample_pos + 0.5) / total_len)
    coeffs = jnp.sinc(centre) * taper_win
    coeffs = coeffs / jnp.sqrt(jnp.sum(coeffs * coeffs))
    return coeffs.reshape(TAPS, NFFT)


def phase_table(left, right, modulus):
    phase_idx = left[:, None] * right[None, :] % modulus
    angles = phase_idx.astype(jnp.float32) * (2.0 * math.pi / modulus)
    return (jnp.cos(angles), jnp.sin(angles))


def transform(row_block):
    best = lax.Precision.HIGHEST
    first_idx = jnp.arange(FA, dtype=jnp.int32)
    second_idx = jnp.arange(FB, dtype=jnp.int32)
    half_idx = jnp.arange(FB // 2, dtype=jnp.int32)
    cos_one, sin_one = phase_table(first_idx, first_idx, FA)
    section_re = jnp.einsum("rab,ak->rkb", row_block, cos_one, precision=best)
    section_im = -jnp.einsum("rab,ak->rkb", row_block, sin_one, precision=best)
    twid_cos, twid_sin = phase_table(first_idx, second_idx, NFFT)
    inner_re = section_re * twid_cos + section_im * twid_sin
    inner_im = section_im * twid_cos - section_re * twid_sin
    cos_two, sin_two = phase_table(second_idx, half_idx, FB)
    freq_re = jnp.einsum("rkb,bq->qkr", inner_re, cos_two, precision=best) + jnp.einsum(
        "rkb,bq->qkr", inner_im, sin_two, precision=best
    )
    freq_im = jnp.einsum("rkb,bq->qkr", inner_im, cos_two, precision=best) - jnp.einsum(
        "rkb,bq->qkr", inner_re, sin_two, precision=best
    )
    row_count = row_block.shape[0]
    return (freq_re.reshape(CH, row_count), freq_im.reshape(CH, row_count))


def plain_shards(voltages, beam_delays, cal_gains):
    inp_dev = voltages.shape[0]
    spec_dev = voltages.shape[1] // NFFT
    tm_count = lax.axis_size("tm")
    chan_count = lax.axis_size("chan")
    spectra_total = spec_dev * tm_count
    raw_block = voltages.reshape(inp_dev, spec_dev, NFFT).transpose(1, 0, 2).astype(jnp.bfloat16)
    tail_block = shifted(raw_block[: TAPS - 1], "tm", -1)
    extended = jnp.concatenate([raw_block, tail_block], axis=0).astype(jnp.float32)
    coeffs = pfb_window()
    filtered = coeffs[0][None, None, :] * extended[0:spec_dev]
    for tap_index in range(1, TAPS):
        filtered = (
            filtered + coeffs[tap_index][None, None, :] * extended[tap_index : tap_index + spec_dev]
        )
    freq_re, freq_im = transform(filtered.reshape(spec_dev * inp_dev, FA, FB))
    packed = (jnp.stack([freq_re, freq_im]) * (1.0 / 64.0)).astype(jnp.bfloat16)
    packed = packed.reshape(2, CH, spec_dev, inp_dev)
    chan_local = CH // (tm_count * chan_count)
    reordered = packed.reshape(2, tm_count, chan_count, chan_local, spec_dev, inp_dev)
    reordered = reordered.transpose(0, 2, 1, 3, 4, 5).reshape(2, CH, spec_dev, inp_dev)
    sectioned = lax.all_to_all(reordered, "chan", split_axis=1, concat_axis=3, tiled=True)
    turned = lax.all_to_all(sectioned, "tm", split_axis=1, concat_axis=2, tiled=True)
    a_re = turned[0].astype(jnp.float32)
    a_im = turned[1].astype(jnp.float32)
    g_re = cal_gains[0][:, None, :]
    g_im = cal_gains[1][:, None, :]
    cal_re = (g_re * a_re - g_im * a_im).astype(jnp.bfloat16)
    cal_im = (g_re * a_im + g_im * a_re).astype(jnp.bfloat16)
    stacked = jnp.concatenate([cal_re, cal_im], axis=1)
    flipped = jnp.concatenate([cal_im, -cal_re], axis=1)
    vis_re = jnp.einsum("ctp,ctq->cpq", stacked, stacked, preferred_element_type=jnp.float32)
    vis_im = jnp.einsum("ctp,ctq->cpq", flipped, stacked, preferred_element_type=jnp.float32)
    visibilities = (jnp.stack([vis_re, vis_im]) / spectra_total).astype(jnp.bfloat16)
    chan_first = (
        lax.axis_index("tm") * (chan_local * chan_count) + lax.axis_index("chan") * chan_local
    )
    chan_ids = chan_first + jnp.arange(chan_local, dtype=jnp.int32)
    phase_idx = beam_delays[None, :, :] * chan_ids[:, None, None] % NFFT
    angles = phase_idx.astype(jnp.float32) * (2.0 * math.pi / NFFT)
    weight_norm = 1.0 / math.sqrt(beam_delays.shape[1])
    weight_re = (jnp.cos(angles) * weight_norm).astype(jnp.bfloat16)
    weight_im = (-jnp.sin(angles) * weight_norm).astype(jnp.bfloat16)
    beam_re = jnp.einsum(
        "cti,cbi->ctb", cal_re, weight_re, preferred_element_type=jnp.float32
    ) - jnp.einsum("cti,cbi->ctb", cal_im, weight_im, preferred_element_type=jnp.float32)
    beam_im = jnp.einsum(
        "cti,cbi->ctb", cal_im, weight_re, preferred_element_type=jnp.float32
    ) + jnp.einsum("cti,cbi->ctb", cal_re, weight_im, preferred_element_type=jnp.float32)
    beam_power = (beam_re * beam_re + beam_im * beam_im).astype(jnp.bfloat16)
    return (visibilities, beam_power)


def solution(mesh):
    return jax.shard_map(
        shards,
        mesh=mesh,
        in_specs=(P(("grp", "chan"), "tm"), P(), P(None, ("grp", "tm", "chan"), None)),
        out_specs=(
            P(None, ("grp", "tm", "chan"), None, None),
            P(("grp", "tm", "chan"), None, None),
        ),
        check_vma=False,
    )
```
